512 devices in a mesh: section: 4 (over x), elem: 128 (over y, z, core).
Axes of the slice: x: 4, y: 8, z: 8, core: 2. Of those that a mesh axis runs over, the one named last changes fastest.
Arguments:
- section_residual: float32 [4, 5, 64, 16384], P('section', None, None, 'elem'), may hold values from -110 to 110
- transform: float32 [4, 4], replicated, may hold values from -0.9 to 3.9
- shifts: float32 [4], P('section'), may hold values from 1 to 4
- linear_flux_matrix: float32 [3, 5, 5, 16384], P(None, None, None, 'elem'), may hold values from -1 to 1
- penalty: float32 [6, 16384], P(None, 'elem'), may hold values from 0.2 to 1
- block_inverse_factor: float32 [4, 5, 5, 16384], P('section', None, None, 'elem'), may hold values from -2.5 to 2.5
- nodal_inverse_factor: float32 [4, 64, 64], P('section'), may hold values from -0.75 to 0.75
- neighbours: int32 [6, 16384], P(None, 'elem'), may hold values from -1 to 16383, as said below
- orientation: int32 [6, 16384], P(None, 'elem'), may hold values from 0 to 7
- live_counts: int32 [128], P('elem'), may hold values from 112 to 128, as said below
Outputs:
- section_update: float32 [4, 5, 64, 16384], P('section', None, None, 'elem')
- start_rms: float32 [4], P('section')
The draws below stay inside these ranges and needn't reach their ends.
Inputs may be any that keep to these rules, and one draw needn't show every extreme that they name: `neighbours`: row f names for face f of element slot g = d * 128 + l the global slot of the element across it, or -1 at walls, at the ends of the slab and for every face of a slot that is not live. Every named slot is live. An element named on another device lies on device d - 1 within its last 32 slots or on device d + 1 within its first 32 slots. Faces f and f xor 1 are opposite, and the relation is symmetric. `live_counts`: live slots of a device come first; the last device is full.
All inputs are finite; a program needn't handle non-finite values.
Results may differ from the reference program's by a relative error of at most 0.0003.
Values sent between devices are 32-bit elements; how exact they have to be, the bound alone decides.
A program may use at most 64 MiB of HBM per device.

```python
import math
import jax
import jax.numpy as jnp
import numpy as np
from jax import lax

SECTIONS = 4
VARS = 5
NODES = 64
ELEM_DEV = 128
STRIDE = 4
ELEMS = 16384
REACH = 16
N_ELEM = 128


def shared_counts(key):
    lowest = ELEM_DEV - ELEM_DEV // 8
    counts = jax.random.randint(key, (N_ELEM,), lowest, ELEM_DEV + 1)
    fullest = jax.random.randint(jax.random.fold_in(key, 7), (), 0, N_ELEM)
    places = jnp.arange(N_ELEM)
    return jnp.where((places == fullest) | (places == N_ELEM - 1), ELEM_DEV, counts).astype(jnp.int32)


def draw_live_counts(key, part):
    return shared_counts(key)


def draw_neighbours(key, part):
    counts = shared_counts(key)
    offsets = jnp.cumsum(counts) - counts
    total = jnp.sum(counts)
    positions = jnp.arange(ELEMS, dtype=jnp.int32)
    device = positions // ELEM_DEV
    local_slot = positions % ELEM_DEV
    live = local_slot < counts[device]
    rank = offsets[device] + local_slot

    def locate(target):
        owner = jnp.sum((offsets[None, :] <= target[:, None]).astype(jnp.int32), axis=1) - 1
        owner = jnp.clip(owner, 0, N_ELEM - 1)
        placed = owner * ELEM_DEV + target - offsets[owner]
        return jnp.where((target >= 0) & (target < total), placed, -1)

    def nearby(offset_by):
        moved = local_slot + offset_by
        inside = (moved >= 0) & (moved < counts[device])
        return jnp.where(inside, device * ELEM_DEV + moved, -1)
    table = jnp.stack([locate(rank - 1), locate(rank + 1), nearby(-STRIDE), nearby(STRIDE), locate(rank - REACH), locate(rank + REACH)])
    return jnp.where(live[None, :], table, -1).astype(jnp.int32)


def draw_section_residual(key, part):
    key = jax.random.fold_in(key, 2)
    keys = jax.random.split(key, 3)
    ramp = jnp.arange(ELEMS, dtype=jnp.float32) / max(ELEMS - 1, 1)
    elem_scale = jnp.exp(jax.random.uniform(keys[0], (ELEMS,), minval=0.0, maxval=1.3862944))
    comp_scale = jnp.exp(jax.random.uniform(keys[1], (VARS, NODES), minval=0.0, maxval=1.0986123))
    base = jnp.clip(jax.random.normal(keys[2], (SECTIONS, VARS, NODES, ELEMS)), -5.0, 5.0)
    growth = jnp.exp(0.5493061 * ramp)
    values = base * (growth * elem_scale)[None, None, None, :] * comp_scale[None, :, :, None]
    return values.astype(jnp.float32)


def draw_transform(key, part):
    key = jax.random.fold_in(key, 3)
    spread_output = jax.random.uniform(key, (SECTIONS, SECTIONS), minval=-0.9, maxval=0.9)
    identity = jnp.eye(SECTIONS, dtype=jnp.float32)
    return 3.0 * identity + spread_output * (1.0 - identity)


def with_ends(values, key, smallest, high):
    place = [jax.random.randint(jax.random.fold_in(key, axis), (), 0, length) for axis, length in enumerate(values.shape)]
    longest = values.shape.index(max(values.shape))
    neighbour = place[:longest] + [(place[longest] + 1) % values.shape[longest]] + place[longest + 1:]
    return values.at[tuple(place)].set(smallest).at[tuple(neighbour)].set(high)


def block_levels(key, dims, cuts, low, top_value):
    def one(position, blocks):
        steps = jax.random.uniform(jax.random.fold_in(jax.random.fold_in(key, 6), position), (blocks,), jnp.float32, low / len(cuts), top_value / len(cuts))
        return jnp.repeat(jnp.exp(steps), dims[position] // blocks).reshape((-1,) + (1,) * (len(dims) - position - 1))

    gain = one(*cuts[0])
    for cut in cuts[1:]:
        gain = gain * one(*cut)
    return gain


def gaussian(rng, dims, width, reach, cuts=(), kind=jnp.bfloat16):
    result = jax.random.normal(rng, dims, jnp.float32) * width
    if len(cuts) > 0:
        result = block_levels(rng, dims, cuts, -0.22, 0.18) * result
    return jnp.clip(result, min=-reach, max=reach).astype(kind)


def setup_inputs(seed: int = 0) -> dict:
    key_list = jax.random.split(jax.random.key(seed), 11)
    return {
        "section_residual": draw_section_residual(jax.random.fold_in(key_list[10], 71), 0),
        "transform": draw_transform(jax.random.fold_in(key_list[10], 71), 0),
        "shifts": jnp.clip(jnp.exp(math.log(4.0) - 1.3862944 * jax.random.uniform(key_list[2], (SECTIONS,), jnp.float32) ** block_levels(key_list[2], (SECTIONS,), ((0, 4),), -0.2, 0.2)), 1.0, 4.0),
        "linear_flux_matrix": gaussian(key_list[3], (3, VARS, VARS, ELEMS), 0.2, 1.0, ((3, 128),), jnp.float32),
        "penalty": jnp.clip(jnp.exp(math.log(1.0) - 1.609438 * jax.random.uniform(key_list[4], (6, ELEMS), jnp.float32) ** block_levels(key_list[4], (6, ELEMS), ((1, 128),), -0.2, 0.2)), 0.2, 1.0),
        "block_inverse_factor": gaussian(key_list[5], (SECTIONS, VARS, VARS, ELEMS), VARS ** -0.5, 2.5, ((0, 4), (3, 128)), jnp.float32),
        "nodal_inverse_factor": gaussian(key_list[6], (SECTIONS, NODES, NODES), NODES ** -0.5, 0.75, ((0, 4),), jnp.float32),
        "neighbours": draw_neighbours(jax.random.fold_in(key_list[10], 71), 0),
        "orientation": with_ends(jax.random.randint(key_list[8], (6, ELEMS), 0, 8), jax.random.fold_in(key_list[8], 1), 0, 7).astype(jnp.int32),
        "live_counts": draw_live_counts(jax.random.fold_in(key_list[10], 71), 0),
    }


TOP_PRECISION = lax.Precision.HIGHEST

def derivative_table():
    points = np.array([-1.0, -np.sqrt(0.2), np.sqrt(0.2), 1.0])
    weights = np.array([1.0 / np.prod([points[column] - points[other_point] for other_point in range(4) if other_point != column]) for column in range(4)])
    table = np.zeros((4, 4))
    for row_at in range(4):
        for column in range(4):
            if row_at != column:
                table[row_at, column] = weights[column] / weights[row_at] / (points[row_at] - points[column])
        table[row_at, row_at] = -np.sum(table[row_at])
    return table

def partner_table():
    corner = np.arange(64).reshape(4, 4, 4)
    face_list = [corner[0], corner[3], corner[:, 0], corner[:, 3], corner[:, :, 0], corner[:, :, 3]]
    partner = np.zeros((6, 8, 16), np.int32)
    for face_id in range(6):
        opposite = face_list[face_id ^ 1]
        for code_id in range(8):
            for place_one in range(4):
                for place_two in range(4):
                    index_one, index_two = (place_one, place_two)
                    if code_id & 4:
                        index_one, index_two = (index_two, index_one)
                    if code_id & 1:
                        index_one = 3 - index_one
                    if code_id & 2:
                        index_two = 3 - index_two
                    partner[face_id, code_id, place_one * 4 + place_two] = opposite[index_one, index_two]
    return partner

def face_selectors():
    full = slice(None)
    return [(full, 0), (full, 3), (full, full, 0), (full, full, 3), (full, full, full, 0), (full, full, full, 3)]

def partner_nodes(orientation):
    code_list = jnp.arange(8, dtype=jnp.int32)
    matches = orientation[:, None, None, :] == code_list[None, :, None, None]
    table = jnp.asarray(partner_table(), dtype=jnp.int32)
    return lax.optimization_barrier(jnp.sum(jnp.where(matches, table[:, :, :, None], 0), axis=1)).astype(jnp.int32)

def invert_small(matrix):
    order_of = matrix.shape[0]
    left_part = matrix
    right_part = jnp.eye(order_of, dtype=matrix.dtype)
    for pivot_at in range(order_of):
        pivot_scale = 1.0 / left_part[pivot_at, pivot_at]
        left_part = left_part.at[pivot_at].multiply(pivot_scale)
        right_part = right_part.at[pivot_at].multiply(pivot_scale)
        for target in range(order_of):
            if target != pivot_at:
                factor = left_part[target, pivot_at]
                left_part = left_part.at[target].add(-factor * left_part[pivot_at])
                right_part = right_part.at[target].add(-factor * right_part[pivot_at])
    return right_part

def operate(source_term, extended, shift_value, linear_flux_matrix, penalty, far_slots, has_partner, node_index, active_mask):
    derivative = jnp.asarray(derivative_table(), dtype=source_term.dtype)
    element_count = source_term.shape[2]
    padded_width = extended.shape[2]
    cube_view = source_term.reshape(5, 4, 4, 4, element_count)
    section_slopes = [jnp.einsum('ai,vijke->vajke', derivative, cube_view, precision=TOP_PRECISION), jnp.einsum('aj,vijke->viake', derivative, cube_view, precision=TOP_PRECISION), jnp.einsum('ak,vijke->vijae', derivative, cube_view, precision=TOP_PRECISION)]
    computed_output = shift_value * source_term
    for axis_direction in range(3):
        computed_output = computed_output + jnp.einsum('kch,cfh->kfh', linear_flux_matrix[axis_direction], section_slopes[axis_direction].reshape(5, 64, element_count), precision=TOP_PRECISION)
    flat_index = (node_index * padded_width + far_slots[:, None, :]).reshape(96 * element_count)
    far_trace = jnp.take(extended.reshape(5, 64 * padded_width), flat_index, axis=1).reshape(5, 6, 16, element_count)
    far_trace = far_trace * has_partner[None, :, None, :]
    result_cube = computed_output.reshape(5, 4, 4, 4, element_count)
    for face_id, selector in enumerate(face_selectors()):
        own_trace = cube_view[selector]
        face_jump = (own_trace - far_trace[:, face_id].reshape(5, 4, 4, element_count)) * penalty[face_id]
        result_cube = result_cube.at[selector].add(face_jump)
    return result_cube.reshape(5, 64, element_count) * active_mask

def precondition(source_term, block_inverse_factor, nodal_inverse_factor, active_mask):
    spread_output = jnp.einsum('ab,cbx->cax', nodal_inverse_factor, source_term, precision=TOP_PRECISION)
    return jnp.einsum('kch,cfh->kfh', block_inverse_factor, spread_output, precision=TOP_PRECISION) * active_mask

def small_solve(start_norm, column_one, column_two):
    top_norm = jnp.sqrt(jnp.sum(column_one * column_one))
    unit_one = column_one / top_norm
    cross_term = jnp.sum(unit_one * column_two)
    remainder = column_two - cross_term * unit_one
    rest_norm = jnp.sqrt(jnp.sum(remainder * remainder))
    coef_two = start_norm * remainder[0] / (rest_norm * rest_norm)
    coef_one = (start_norm * unit_one[0] - cross_term * coef_two) / top_norm
    return (coef_one, coef_two)

def krylov_solve(right_side, apply_operator, apply_precond):
    start_norm = jnp.sqrt(jnp.sum(right_side * right_side))
    krylov_basis = [right_side / start_norm]
    directions = []
    columns = []
    for column in range(2):
        axis_direction = apply_precond(krylov_basis[column])
        directions.append(axis_direction)
        mapped = apply_operator(axis_direction)
        coefficients = [jnp.sum(mapped * vector) for vector in krylov_basis]
        for coefficient, vector in zip(coefficients, krylov_basis):
            mapped = mapped - coefficient * vector
        length = jnp.sqrt(jnp.sum(mapped * mapped))
        krylov_basis.append(mapped / length)
        columns.append(coefficients + [length])
    column_one = jnp.stack(columns[0] + [jnp.zeros_like(start_norm)])
    column_two = jnp.stack(columns[1])
    coef_one, coef_two = small_solve(start_norm, column_one, column_two)
    return (coef_one * directions[0] + coef_two * directions[1], start_norm)

def reference(section_residual, transform, shifts, linear_flux_matrix, penalty, block_inverse_factor, nodal_inverse_factor, neighbours, orientation, live_counts):
    element_count = section_residual.shape[3]
    positions = jnp.arange(element_count, dtype=jnp.int32)
    device = positions // ELEM_DEV
    local_slot = positions % ELEM_DEV
    active_mask = (local_slot < live_counts[device]).astype(section_residual.dtype)
    inverse = invert_small(transform)
    mixed_rhs = jnp.einsum('st,tvne->svne', inverse, section_residual, precision=TOP_PRECISION) * active_mask
    has_partner = (neighbours >= 0).astype(section_residual.dtype)
    far_slots = jnp.maximum(neighbours, 0).astype(jnp.int32)
    node_index = partner_nodes(orientation)
    solved = []
    norms = []
    for section_id in range(SECTIONS):

        def apply_operator(source_term, section_id=section_id):
            return operate(source_term, source_term, shifts[section_id], linear_flux_matrix, penalty, far_slots, has_partner, node_index, active_mask)

        def apply_precond(source_term, section_id=section_id):
            return precondition(source_term, block_inverse_factor[section_id], nodal_inverse_factor[section_id], active_mask)
        result_value, norm_value = krylov_solve(mixed_rhs[section_id], apply_operator, apply_precond)
        solved.append(result_value)
        norms.append(norm_value)
    solution = jnp.stack(solved)
    start_rms = jnp.stack(norms) / jnp.sqrt(jnp.asarray(VARS * NODES * ELEMS, dtype=section_residual.dtype))
    return (jnp.einsum('st,tvne->svne', transform, solution, precision=TOP_PRECISION), start_rms)
```

```python
import functools

import jax
import jax.numpy as jnp
import numpy as np
from jax import lax
from jax.experimental import pallas as pl
from jax.experimental.pallas import tpu as pltpu
from jax.sharding import PartitionSpec as P

MESH = pl.DeviceIdType.MESH
F32 = jnp.float32
I32 = jnp.int32
VARS, NODES, LANES, HALO = 5, 64, 128, 32
SECTIONS, ROW, COLS = 4, 16, 8


def derivative_table():
    points = np.array([-1.0, -np.sqrt(0.2), np.sqrt(0.2), 1.0])
    weights = np.array([1.0 / np.prod([points[b] - points[c] for c in range(4) if c != b]) for b in range(4)])
    table = np.zeros((4, 4))
    for a in range(4):
        for b in range(4):
            if a != b:
                table[a, b] = weights[b] / weights[a] / (points[a] - points[b])
        table[a, a] = -np.sum(table[a])
    return table


def slope_matrix():
    table, eye = derivative_table().astype(np.float32).astype(np.float64), np.eye(4)
    parts = [np.eye(NODES)]
    for spots in ((table, eye, eye), (eye, table, eye), (eye, eye, table)):
        parts.append(np.kron(np.kron(spots[0], spots[1]), spots[2]))
    return np.concatenate(parts).astype(np.float32)


def dot(a, b):
    return jnp.dot(a, b, precision=lax.Precision.HIGHEST, preferred_element_type=F32)


def inverse_of(entries):
    left = [[entries[i][j] for j in range(4)] for i in range(4)]
    right = [[jnp.full_like(entries[0][0], 1.0 if i == j else 0.0) for j in range(4)] for i in range(4)]
    for pivot in range(4):
        scale = 1.0 / left[pivot][pivot]
        left[pivot] = [x * scale for x in left[pivot]]
        right[pivot] = [x * scale for x in right[pivot]]
        for target in range(4):
            if target != pivot:
                factor = left[target][pivot]
                left[target] = [x - factor * y for x, y in zip(left[target], left[pivot])]
                right[target] = [x - factor * y for x, y in zip(right[target], right[pivot])]
    return right


def pick(choices, which):
    out = choices[0]
    for i in range(1, len(choices)):
        out = jnp.where(which == i, choices[i], out)
    return out


def face_rows(u):
    sub = lax.broadcasted_iota(I32, (8, LANES), 0)
    low = sub < 4
    rows = [[u[0][0], u[0][1]], [u[3][0], u[3][1]], [], [], [], []]
    for h in range(2):
        a, b = u[2 * h], u[2 * h + 1]
        rows[2].append(jnp.where(low, a[0], pltpu.roll(b[0], 4, 0)))
        rows[3].append(jnp.where(low, pltpu.roll(a[1], 4, 0), b[1]))
    for f, k in ((4, 0), (5, 3)):
        at = k + 4 * (sub & 1)
        for h in range(2):
            a, b = u[2 * h], u[2 * h + 1]
            s = [jnp.take_along_axis(x, at, axis=0) for x in (a[0], a[1], b[0], b[1])]
            rows[f].append(jnp.where(low, jnp.where(sub < 2, s[0], s[1]), jnp.where(sub < 6, s[2], s[3])))
    return rows


def turned(a, b, code):
    swap = (code & 4) != 0
    a2 = jnp.where(swap, b, a)
    b2 = jnp.where(swap, a, b)
    a2 = jnp.where((code & 1) != 0, 3 - a2, a2)
    b2 = jnp.where((code & 2) != 0, 3 - b2, b2)
    return 4 * a2 + b2


def body(
    residual, transform, shifts, flux, penalty, block_inverse, nodal_inverse, neighbours, orientation, live_counts, slopes,
    out, rms,
    v_res, v_flux, v_pen, v_block, v_nodal, v_neigh, v_orient, v_slopes, s_transform, s_shift, s_live,
    n_all, mixed, blocks, pen_node, far_coef, far_row, own_at, halo_at, y, r, w, dirs, faces, near, pack, halo, red1, red2,
    in_sem, res_send, res_recv, dir_send, dir_recv, halo_send, halo_recv, red_send, red_recv,
):
    s, e = lax.axis_index("section"), lax.axis_index("elem")
    x_peers = [(lax.rem(s + k, SECTIONS), e) for k in (1, 3, 2)]
    nxt, prv = (s, lax.rem(e + 1, 128)), (s, lax.rem(e + 127, 128))
    row_base = (e // ROW) * ROW
    row_at = e - row_base
    row_peers = [(s, row_base + lax.rem(row_at + k, ROW)) for k in (8, 9, 7, 6, 10, 5, 11, 4, 12, 3, 13, 2, 14, 15, 1)]
    plane_at = s * COLS + e // ROW
    plane_peers = []
    for k in (2, 1, 3, 0):
        for q in (4, 3, 5, 2, 6, 1, 7, 0):
            if k or q:
                plane_peers.append((lax.rem(s + k, SECTIONS), lax.rem(e + ROW * q, 128)))

    barrier = pltpu.get_barrier_semaphore()
    peers = x_peers + [nxt, prv] + row_peers + plane_peers
    for p in peers:
        pl.semaphore_signal(barrier, inc=1, device_id=p, device_id_type=MESH)

    loads = [
        (residual.at[0], v_res.at[s]), (flux, v_flux), (penalty, v_pen), (block_inverse.at[0], v_block), (nodal_inverse.at[0], v_nodal),
        (neighbours, v_neigh), (orientation, v_orient), (slopes, v_slopes), (transform, s_transform), (shifts, s_shift),
        (live_counts, s_live),
    ]
    loads = [pltpu.make_async_copy(a, b, in_sem.at[i]) for i, (a, b) in enumerate(loads)]
    for c in loads:
        c.start()

    pl.semaphore_wait(barrier, len(peers))
    res_copies = []
    for j, p in enumerate(x_peers):
        c = pltpu.make_async_remote_copy(
            src_ref=residual.at[0], dst_ref=v_res.at[s], send_sem=res_send.at[j], recv_sem=res_recv.at[j], device_id=p,
            device_id_type=MESH,
        )
        c.start()
        res_copies.append(c)
    for c in loads:
        c.wait()

    lane = lax.broadcasted_iota(I32, (8, LANES), 1)
    sub = lax.broadcasted_iota(I32, (8, LANES), 0)
    mask = jnp.where(lane < s_live[0], 1.0, 0.0).astype(F32)
    mask1 = mask[0:1]
    t_entries = [[jnp.full((8, LANES), s_transform[i, j], F32) for j in range(4)] for i in range(4)]
    inverse = inverse_of(t_entries)
    mix = [pick([inverse[i][t] for i in range(4)], s) * mask for t in range(4)]
    t_row = [pick([t_entries[i][t] for i in range(4)], s) for t in range(4)]

    n_all[...] = dot(v_slopes[...], v_nodal[...])
    for m in range(VARS):
        blocks[m] = v_block[m] * mask1
    for d in range(3):
        for k in range(VARS):
            total = None
            for m in range(VARS):
                term = v_flux[d, k, m:m + 1, :] * blocks[m]
                total = term if total is None else total + term
            mixed[d, k] = total

    dead = jnp.zeros((8, LANES), F32)
    coef, code = [], []
    for f in range(6):
        far = jnp.broadcast_to(v_neigh[f:f + 1, :], (8, LANES))
        there = far >= 0
        at = far - e * LANES
        inside = there & (at >= 0) & (at < LANES)
        before = there & (at < 0)
        after = there & (at >= LANES)
        own_at[f] = jnp.where(inside, at, 0)
        halo_at[f] = jnp.where(before, at + HALO, jnp.where(after, at - LANES, 0))
        halo_at[6 + f] = jnp.where(before, 1, jnp.where(after, 2, 0))
        coef.append(jnp.where(there, jnp.broadcast_to(v_pen[f:f + 1, :], (8, LANES)), dead) * mask)
        code.append(jnp.broadcast_to(v_orient[f:f + 1, :], (8, LANES)))
    k_at, j_low = sub & 3, sub >> 2
    for n, (i, jh) in enumerate(((0, 0), (0, 1), (3, 0), (3, 1))):
        f = 0 if i == 0 else 1
        far_coef[n] = coef[f]
        far_row[n] = turned(2 * jh + j_low, k_at, code[f])
    for i in range(4):
        for jh in range(2):
            n = 4 + 2 * i + jh
            f = 2 + jh
            far_coef[n] = jnp.where(j_low == jh, coef[f], dead)
            far_row[n] = turned(jnp.full((8, LANES), i, I32), k_at, code[f])
            n += 8
            low_face = k_at < 2
            far_coef[n] = jnp.where(k_at == 0, coef[4], jnp.where(k_at == 3, coef[5], dead))
            far_row[n] = turned(jnp.full((8, LANES), i, I32), 2 * jh + j_low, jnp.where(low_face, code[4], code[5]))
    own_pen = [jnp.broadcast_to(v_pen[f:f + 1, :], (8, LANES)) for f in range(6)]
    for i in range(4):
        for jh in range(2):
            total = jnp.full((8, LANES), s_shift[0], F32)
            if i in (0, 3):
                total = total + own_pen[0 if i == 0 else 1]
            total = total + jnp.where(j_low == jh, own_pen[2 + jh], dead)
            total = total + jnp.where(k_at == 0, own_pen[4], jnp.where(k_at == 3, own_pen[5], dead))
            pen_node[2 * i + jh] = total

    for c in res_copies:
        c.wait_recv()
    for k in range(VARS):
        for q in range(8):
            rows = pl.ds(8 * q, 8)
            total = mix[0] * v_res[0, k, rows, :]
            for t in range(1, 4):
                total = total + mix[t] * v_res[t, k, rows, :]
            r[k, rows, :] = total

    dir_copies, halo_copies = [], []

    def operator(step, source, target):
        for k in range(VARS):
            y[k] = dot(n_all[...], source[k])
        for k in range(VARS):
            total = None
            for c in range(VARS):
                term = blocks[k, c:c + 1, :] * y[c, 0:NODES, :]
                total = term if total is None else total + term
            dirs[step, s, k] = total
        for k in range(VARS):
            u = [[dirs[step, s, k, pl.ds(16 * i + 8 * jh, 8), :] for jh in range(2)] for i in range(4)]
            rows = face_rows(u)
            for f in range(6):
                for h in range(2):
                    faces[f * 10 + k * 2 + h] = rows[f][h]
        group = lane >> 5
        for p in range(15):
            x = [faces[4 * p + g] for g in range(4)]
            x = [x[0]] + [pltpu.roll(x[g], 32 * g, 1) for g in range(1, 4)]
            pack[step, 0, p] = jnp.where(group < 2, jnp.where(group == 0, x[0], x[1]), jnp.where(group == 2, x[2], x[3]))
            pack[step, 1, p] = jnp.where(group < 2, jnp.where(group == 0, x[1], x[2]), jnp.where(group == 2, x[3], x[0]))
        waits = []
        for side, p in ((0, prv), (1, nxt)):
            c = pltpu.make_async_remote_copy(
                src_ref=pack.at[step, side], dst_ref=halo.at[step, side], send_sem=halo_send.at[step, side],
                recv_sem=halo_recv.at[step, side], device_id=p, device_id_type=MESH,
            )
            c.start()
            waits.append(c)
            halo_copies.append(c)
        for j, p in enumerate(x_peers):
            c = pltpu.make_async_remote_copy(
                src_ref=dirs.at[step, s], dst_ref=dirs.at[step, s], send_sem=dir_send.at[step, j],
                recv_sem=dir_recv.at[step, j], device_id=p, device_id_type=MESH,
            )
            c.start()
            dir_copies.append(c)
        for k in range(VARS):
            total = jnp.concatenate([pen_node[q] for q in range(8)], axis=0) * dirs[step, s, k]
            for d in range(3):
                for c in range(VARS):
                    total = total + mixed[d, k, c:c + 1, :] * y[c, NODES * (d + 1):NODES * (d + 2), :]
            target[k] = total
        for f in range(6):
            at = own_at[f]
            for n in range(10):
                near[f * 10 + n] = jnp.take_along_axis(faces[(f ^ 1) * 10 + n], at, axis=1)
        for c in waits:
            c.wait_recv()
        for f in range(6):
            at = halo_at[f]
            side = halo_at[6 + f]
            for n in range(10):
                m = (f ^ 1) * 10 + n
                p, g = m // 4, m % 4
                after = jnp.take_along_axis(halo[step, 0, p], at + 32 * g, axis=1)
                before = jnp.take_along_axis(halo[step, 1, p], at + 32 * ((g + 3) % 4), axis=1)
                near[f * 10 + n] = jnp.where(side == 0, near[f * 10 + n], jnp.where(side == 1, before, after))
        for n in range(20):
            row = far_row[n]
            at, high = row & 7, row >= 8
            if n < 4:
                f, i, jh = n // 2, 3 * (n // 2), n % 2
            else:
                i, jh = ((n - 4) % 8) // 2, n % 2
                f = 2 + jh if n < 12 else 4
            for k in range(VARS):
                def turn(face):
                    a = jnp.take_along_axis(near[face * 10 + 2 * k], at, axis=0)
                    b = jnp.take_along_axis(near[face * 10 + 2 * k + 1], at, axis=0)
                    return jnp.where(high, b, a)

                far = turn(f) if f < 4 else jnp.where(k_at < 2, turn(4), turn(5))
                rows = pl.ds(16 * i + 8 * jh, 8)
                target[k, rows, :] = target[k, rows, :] - far_coef[n] * far

    operator(0, r, w.at[0])
    operator(1, w.at[0], w.at[1])

    sums = [None] * 6
    for k in range(VARS):
        for q in range(8):
            rows = pl.ds(8 * q, 8)
            a, b, c = r[k, rows, :], w[0, k, rows, :], w[1, k, rows, :]
            for n, term in enumerate((a * a, a * b, b * b, a * c, b * c, c * c)):
                sums[n] = term if sums[n] is None else sums[n] + term
    stacked = dead
    for n in range(6):
        stacked = jnp.where(sub == n, jnp.sum(sums[n], axis=0, keepdims=True), stacked)
    stacked = jnp.where(sub == lane, jnp.sum(stacked, axis=1, keepdims=True), dead)
    red1[row_at] = jnp.sum(stacked, axis=0, keepdims=True)
    for p in row_peers:
        pltpu.make_async_remote_copy(
            src_ref=red1.at[row_at], dst_ref=red1.at[row_at], send_sem=red_send.at[0], recv_sem=red_recv.at[0], device_id=p,
            device_id_type=MESH,
        ).start()
    all_row = pltpu.make_async_remote_copy(
        src_ref=red1.at[pl.ds(0, ROW - 1)], dst_ref=red1.at[pl.ds(0, ROW - 1)], send_sem=red_send.at[0],
        recv_sem=red_recv.at[0], device_id=prv, device_id_type=MESH,
    )
    all_row.wait_recv()
    total = red1[0]
    for n in range(1, ROW):
        total = total + red1[n]
    red2[plane_at] = total
    for p in plane_peers:
        pltpu.make_async_remote_copy(
            src_ref=red2.at[plane_at], dst_ref=red2.at[plane_at], send_sem=red_send.at[1], recv_sem=red_recv.at[1],
            device_id=p, device_id_type=MESH,
        ).start()
    count = SECTIONS * COLS - 1
    all_plane = pltpu.make_async_remote_copy(
        src_ref=red2.at[pl.ds(0, count)], dst_ref=red2.at[pl.ds(0, count)], send_sem=red_send.at[1],
        recv_sem=red_recv.at[1], device_id=prv, device_id_type=MESH,
    )
    all_plane.wait_recv()
    one, two = [], []
    start = None
    for t in range(SECTIONS):
        total = red2[COLS * t]
        for n in range(1, COLS):
            total = total + red2[COLS * t + n]
        g = [jnp.sum(jnp.where(lane[0:1] == n, total, 0.0), axis=1, keepdims=True) for n in range(6)]
        ratio = g[4] / g[2]
        c2 = (g[3] - ratio * g[1]) / (g[5] - ratio * g[4])
        c1 = g[1] / g[2] - ratio * c2
        one.append(t_row[t] * c1)
        two.append(t_row[t] * c2)
        start = g[0] if start is None else jnp.where(s == t, g[0], start)
    rms[...] = jnp.broadcast_to(jnp.sqrt(start) / np.float32(np.sqrt(np.float32(VARS * NODES * LANES * 128))), rms.shape)
    for c in dir_copies:
        c.wait_recv()
    for k in range(VARS):
        for q in range(8):
            rows = pl.ds(8 * q, 8)
            total = None
            for t in range(SECTIONS):
                term = one[t] * dirs[0, t, k, rows, :] + two[t] * dirs[1, t, k, rows, :]
                total = term if total is None else total + term
            out[0, k, rows, :] = total
    for c in res_copies + dir_copies + halo_copies + [all_row, all_plane]:
        c.wait_send()


def local(*args):
    hbm = pl.BlockSpec(memory_space=pl.ANY)
    vmem = pl.BlockSpec(memory_space=pltpu.VMEM)
    dma = pltpu.SemaphoreType.DMA
    slopes = jnp.asarray(slope_matrix())
    update, rms = pl.pallas_call(
        body,
        out_shape=(
            jax.ShapeDtypeStruct((1, VARS, NODES, LANES), F32),
            jax.ShapeDtypeStruct((1, LANES), F32),
        ),
        in_specs=[hbm] * 11,
        out_specs=(vmem, vmem),
        scratch_shapes=[
            pltpu.VMEM((SECTIONS, VARS, NODES, LANES), F32),
            pltpu.VMEM((3, VARS, VARS, LANES), F32),
            pltpu.VMEM((6, LANES), F32),
            pltpu.VMEM((VARS, VARS, LANES), F32),
            pltpu.VMEM((NODES, NODES), F32),
            pltpu.VMEM((6, LANES), I32),
            pltpu.VMEM((6, LANES), I32),
            pltpu.VMEM((4 * NODES, NODES), F32),
            pltpu.SMEM((4, 4), F32),
            pltpu.SMEM((1,), F32),
            pltpu.SMEM((1,), I32),
            pltpu.VMEM((4 * NODES, NODES), F32),
            pltpu.VMEM((3, VARS, VARS, LANES), F32),
            pltpu.VMEM((VARS, VARS, LANES), F32),
            pltpu.VMEM((8, 8, LANES), F32),
            pltpu.VMEM((20, 8, LANES), F32),
            pltpu.VMEM((20, 8, LANES), I32),
            pltpu.VMEM((6, 8, LANES), I32),
            pltpu.VMEM((12, 8, LANES), I32),
            pltpu.VMEM((VARS, 4 * NODES, LANES), F32),
            pltpu.VMEM((VARS, NODES, LANES), F32),
            pltpu.VMEM((2, VARS, NODES, LANES), F32),
            pltpu.VMEM((2, SECTIONS, VARS, NODES, LANES), F32),
            pltpu.VMEM((60, 8, LANES), F32),
            pltpu.VMEM((60, 8, LANES), F32),
            pltpu.VMEM((2, 2, 15, 8, LANES), F32),
            pltpu.VMEM((2, 2, 15, 8, LANES), F32),
            pltpu.VMEM((ROW, 1, LANES), F32),
            pltpu.VMEM((SECTIONS * COLS, 1, LANES), F32),
            dma((11,)), dma((3,)), dma((3,)), dma((2, 3)), dma((2, 3)), dma((2, 2)), dma((2, 2)), dma((2,)), dma((2,)),
        ],
        compiler_params=pltpu.CompilerParams(collective_id=0, has_side_effects=True, vmem_limit_bytes=32 * 1024 * 1024),
        name="newton_step",
    )(*args, slopes)
    return update, rms[0, 0:1]


def solution(mesh):
    placed = (
        P("section", None, None, "elem"), P(), P("section"), P(None, None, None, "elem"), P(None, "elem"),
        P("section", None, None, "elem"), P("section", None, None), P(None, "elem"), P(None, "elem"), P("elem"),
    )
    return jax.shard_map(
        local, mesh=mesh, in_specs=placed, out_specs=(P("section", None, None, "elem"), P("section")), check_vma=False,
    )
```

```python
import functools

import jax
import jax.numpy as jnp
import numpy as np
from jax import lax
from jax.experimental import pallas as pl
from jax.experimental.pallas import tpu as pltpu
from jax.sharding import PartitionSpec as P

MESH = pl.DeviceIdType.MESH
F32 = jnp.float32
I32 = jnp.int32
VARS, NODES, LANES, HALO = 5, 64, 128, 32
SECTIONS, ROW, COLS = 4, 16, 8


def derivative_table():
    points = np.array([-1.0, -np.sqrt(0.2), np.sqrt(0.2), 1.0])
    weights = np.array([1.0 / np.prod([points[b] - points[c] for c in range(4) if c != b]) for b in range(4)])
    table = np.zeros((4, 4))
    for a in range(4):
        for b in range(4):
            if a != b:
                table[a, b] = weights[b] / weights[a] / (points[a] - points[b])
        table[a, a] = -np.sum(table[a])
    return table


def slope_matrix():
    table, eye = derivative_table().astype(np.float32).astype(np.float64), np.eye(4)
    parts = [np.eye(NODES)]
    for spots in ((table, eye, eye), (eye, table, eye), (eye, eye, table)):
        parts.append(np.kron(np.kron(spots[0], spots[1]), spots[2]))
    return np.concatenate(parts).astype(np.float32)


def dot(a, b):
    return jnp.dot(a, b, precision=lax.Precision.HIGHEST, preferred_element_type=F32)


def inverse_of(entries):
    left = [[entries[i][j] for j in range(4)] for i in range(4)]
    right = [[jnp.full_like(entries[0][0], 1.0 if i == j else 0.0) for j in range(4)] for i in range(4)]
    for pivot in range(4):
        scale = 1.0 / left[pivot][pivot]
        left[pivot] = [x * scale for x in left[pivot]]
        right[pivot] = [x * scale for x in right[pivot]]
        for target in range(4):
            if target != pivot:
                factor = left[target][pivot]
                left[target] = [x - factor * y for x, y in zip(left[target], left[pivot])]
                right[target] = [x - factor * y for x, y in zip(right[target], right[pivot])]
    return right


def pick(choices, which):
    out = choices[0]
    for i in range(1, len(choices)):
        out = jnp.where(which == i, choices[i], out)
    return out


def face_rows(u):
    sub = lax.broadcasted_iota(I32, (8, LANES), 0)
    low = sub < 4
    rows = [[u[0][0], u[0][1]], [u[3][0], u[3][1]], [], [], [], []]
    for h in range(2):
        a, b = u[2 * h], u[2 * h + 1]
        rows[2].append(jnp.where(low, a[0], pltpu.roll(b[0], 4, 0)))
        rows[3].append(jnp.where(low, pltpu.roll(a[1], 4, 0), b[1]))
    for f, k in ((4, 0), (5, 3)):
        at = k + 4 * (sub & 1)
        for h in range(2):
            a, b = u[2 * h], u[2 * h + 1]
            s = [jnp.take_along_axis(x, at, axis=0) for x in (a[0], a[1], b[0], b[1])]
            rows[f].append(jnp.where(low, jnp.where(sub < 2, s[0], s[1]), jnp.where(sub < 6, s[2], s[3])))
    return rows


def turned(a, b, code):
    swap = (code & 4) != 0
    a2 = jnp.where(swap, b, a)
    b2 = jnp.where(swap, a, b)
    a2 = jnp.where((code & 1) != 0, 3 - a2, a2)
    b2 = jnp.where((code & 2) != 0, 3 - b2, b2)
    return 4 * a2 + b2


def body(
    residual, transform, shifts, flux, penalty, block_inverse, nodal_inverse, neighbours, orientation, live_counts, slopes,
    out, rms,
    v_res, v_flux, v_pen, v_block, v_nodal, v_neigh, v_orient, v_slopes, s_transform, s_shift, s_live,
    n_all, mixed, blocks, pen_node, far_coef, far_row, own_at, halo_at, y, r, w, dirs, faces, near, pack, halo, red1, red2,
    in_sem, res_send, res_recv, dir_send, dir_recv, halo_send, halo_recv, red_send, red_recv,
):
    s, e = lax.axis_index("section"), lax.axis_index("elem")
    x_peers = [(lax.rem(s + k, SECTIONS), e) for k in (1, 3, 2)]
    nxt, prv = (s, lax.rem(e + 1, 128)), (s, lax.rem(e + 127, 128))
    row_base = (e // ROW) * ROW
    row_at = e - row_base
    row_peers = [(s, row_base + lax.rem(row_at + k, ROW)) for k in (8, 9, 7, 6, 10, 5, 11, 4, 12, 3, 13, 2, 14, 15, 1)]
    plane_at = s * COLS + e // ROW
    plane_peers = []
    for k in (2, 1, 3, 0):
        for q in (4, 3, 5, 2, 6, 1, 7, 0):
            if k or q:
                plane_peers.append((lax.rem(s + k, SECTIONS), lax.rem(e + ROW * q, 128)))

    barrier = pltpu.get_barrier_semaphore()
    peers = x_peers + [nxt, prv] + row_peers + plane_peers
    for p in peers:
        pl.semaphore_signal(barrier, inc=1, device_id=p, device_id_type=MESH)

    loads = [
        (residual.at[0], v_res.at[s]), (flux, v_flux), (penalty, v_pen), (block_inverse, v_block), (nodal_inverse.at[0], v_nodal),
        (neighbours, v_neigh), (orientation, v_orient), (slopes, v_slopes), (transform, s_transform), (shifts, s_shift),
        (live_counts, s_live),
    ]
    loads = [pltpu.make_async_copy(a, b, in_sem.at[i]) for i, (a, b) in enumerate(loads)]
    for c in loads:
        c.start()

    pl.semaphore_wait(barrier, len(peers))
    res_copies = []
    for j, p in enumerate(x_peers):
        c = pltpu.make_async_remote_copy(
            src_ref=residual.at[0], dst_ref=v_res.at[s], send_sem=res_send.at[j], recv_sem=res_recv.at[j], device_id=p,
            device_id_type=MESH,
        )
        c.start()
        res_copies.append(c)
    for c in loads:
        c.wait()

    lane = lax.broadcasted_iota(I32, (8, LANES), 1)
    sub = lax.broadcasted_iota(I32, (8, LANES), 0)
    mask = jnp.where(lane < s_live[0], 1.0, 0.0).astype(F32)
    mask1 = mask[0:1]
    t_entries = [[jnp.full((8, LANES), s_transform[i, j], F32) for j in range(4)] for i in range(4)]
    inverse = inverse_of(t_entries)
    mix = [pick([inverse[i][t] for i in range(4)], s) * mask for t in range(4)]
    t_row = [pick([t_entries[i][t] for i in range(4)], s) for t in range(4)]

    n_all[...] = dot(v_slopes[...], v_nodal[...])
    for m in range(VARS):
        blocks[m] = jnp.concatenate([v_block[m, c] for c in range(VARS)], axis=0) * mask1
    for d in range(3):
        for k in range(VARS):
            total = None
            for m in range(VARS):
                term = v_flux[k, m, d:d + 1, :] * blocks[m]
                total = term if total is None else total + term
            mixed[d, k] = total

    dead = jnp.zeros((8, LANES), F32)
    coef, code = [], []
    for f in range(6):
        far = jnp.broadcast_to(v_neigh[f:f + 1, :], (8, LANES))
        there = far >= 0
        at = far - e * LANES
        inside = there & (at >= 0) & (at < LANES)
        before = there & (at < 0)
        after = there & (at >= LANES)
        own_at[f] = jnp.where(inside, at, 0)
        halo_at[f] = jnp.where(before, at + HALO, jnp.where(after, at - LANES, 0))
        halo_at[6 + f] = jnp.where(before, 1, jnp.where(after, 2, 0))
        coef.append(jnp.where(there, jnp.broadcast_to(v_pen[f:f + 1, :], (8, LANES)), dead) * mask)
        code.append(jnp.broadcast_to(v_orient[f:f + 1, :], (8, LANES)))
    k_at, j_low = sub & 3, sub >> 2
    for n, (i, jh) in enumerate(((0, 0), (0, 1), (3, 0), (3, 1))):
        f = 0 if i == 0 else 1
        far_coef[n] = coef[f]
        far_row[n] = turned(2 * jh + j_low, k_at, code[f])
    for i in range(4):
        for jh in range(2):
            n = 4 + 2 * i + jh
            f = 2 + jh
            far_coef[n] = jnp.where(j_low == jh, coef[f], dead)
            far_row[n] = turned(jnp.full((8, LANES), i, I32), k_at, code[f])
            n += 8
            low_face = k_at < 2
            far_coef[n] = jnp.where(k_at == 0, coef[4], jnp.where(k_at == 3, coef[5], dead))
            far_row[n] = turned(jnp.full((8, LANES), i, I32), 2 * jh + j_low, jnp.where(low_face, code[4], code[5]))
    own_pen = [jnp.broadcast_to(v_pen[f:f + 1, :], (8, LANES)) for f in range(6)]
    for i in range(4):
        for jh in range(2):
            total = jnp.full((8, LANES), s_shift[0], F32)
            if i in (0, 3):
                total = total + own_pen[0 if i == 0 else 1]
            total = total + jnp.where(j_low == jh, own_pen[2 + jh], dead)
            total = total + jnp.where(k_at == 0, own_pen[4], jnp.where(k_at == 3, own_pen[5], dead))
            pen_node[2 * i + jh] = total

    for c in res_copies:
        c.wait_recv()
    for k in range(VARS):
        for q in range(8):
            rows = pl.ds(8 * q, 8)
            total = mix[0] * v_res[0, k, rows, :]
            for t in range(1, 4):
                total = total + mix[t] * v_res[t, k, rows, :]
            r[k, rows, :] = total

    dir_copies, halo_copies = [], []

    def operator(step, source, target):
        for k in range(VARS):
            y[k] = dot(n_all[...], source[k])
        for k in range(VARS):
            total = None
            for c in range(VARS):
                term = blocks[k, c:c + 1, :] * y[c, 0:NODES, :]
                total = term if total is None else total + term
            dirs[step, s, k] = total
        for k in range(VARS):
            u = [[dirs[step, s, k, pl.ds(16 * i + 8 * jh, 8), :] for jh in range(2)] for i in range(4)]
            rows = face_rows(u)
            for f in range(6):
                for h in range(2):
                    faces[f * 10 + k * 2 + h] = rows[f][h]
        group = lane >> 5
        for p in range(15):
            x = [faces[4 * p + g] for g in range(4)]
            x = [x[0]] + [pltpu.roll(x[g], 32 * g, 1) for g in range(1, 4)]
            pack[step, 0, p] = jnp.where(group < 2, jnp.where(group == 0, x[0], x[1]), jnp.where(group == 2, x[2], x[3]))
            pack[step, 1, p] = jnp.where(group < 2, jnp.where(group == 0, x[1], x[2]), jnp.where(group == 2, x[3], x[0]))
        waits = []
        for side, p in ((0, prv), (1, nxt)):
            c = pltpu.make_async_remote_copy(
                src_ref=pack.at[step, side], dst_ref=halo.at[step, side], send_sem=halo_send.at[step, side],
                recv_sem=halo_recv.at[step, side], device_id=p, device_id_type=MESH,
            )
            c.start()
            waits.append(c)
            halo_copies.append(c)
        for j, p in enumerate(x_peers):
            c = pltpu.make_async_remote_copy(
                src_ref=dirs.at[step, s], dst_ref=dirs.at[step, s], send_sem=dir_send.at[step, j],
                recv_sem=dir_recv.at[step, j], device_id=p, device_id_type=MESH,
            )
            c.start()
            dir_copies.append(c)
        for k in range(VARS):
            total = jnp.concatenate([pen_node[q] for q in range(8)], axis=0) * dirs[step, s, k]
            for d in range(3):
                for c in range(VARS):
                    total = total + mixed[d, k, c:c + 1, :] * y[c, NODES * (d + 1):NODES * (d + 2), :]
            target[k] = total
        for f in range(6):
            at = own_at[f]
            for n in range(10):
                near[f * 10 + n] = jnp.take_along_axis(faces[(f ^ 1) * 10 + n], at, axis=1)
        for c in waits:
            c.wait_recv()
        for f in range(6):
            at = halo_at[f]
            side = halo_at[6 + f]
            for n in range(10):
                m = (f ^ 1) * 10 + n
                p, g = m // 4, m % 4
                after = jnp.take_along_axis(halo[step, 0, p], at + 32 * g, axis=1)
                before = jnp.take_along_axis(halo[step, 1, p], at + 32 * ((g + 3) % 4), axis=1)
                near[f * 10 + n] = jnp.where(side == 0, near[f * 10 + n], jnp.where(side == 1, before, after))
        for n in range(20):
            row = far_row[n]
            at, high = row & 7, row >= 8
            if n < 4:
                f, i, jh = n // 2, 3 * (n // 2), n % 2
            else:
                i, jh = ((n - 4) % 8) // 2, n % 2
                f = 2 + jh if n < 12 else 4
            for k in range(VARS):
                def turn(face):
                    a = jnp.take_along_axis(near[face * 10 + 2 * k], at, axis=0)
                    b = jnp.take_along_axis(near[face * 10 + 2 * k + 1], at, axis=0)
                    return jnp.where(high, b, a)

                far = turn(f) if f < 4 else jnp.where(k_at < 2, turn(4), turn(5))
                rows = pl.ds(16 * i + 8 * jh, 8)
                target[k, rows, :] = target[k, rows, :] - far_coef[n] * far

    operator(0, r, w.at[0])
    operator(1, w.at[0], w.at[1])

    sums = [None] * 6
    for k in range(VARS):
        for q in range(8):
            rows = pl.ds(8 * q, 8)
            a, b, c = r[k, rows, :], w[0, k, rows, :], w[1, k, rows, :]
            for n, term in enumerate((a * a, a * b, b * b, a * c, b * c, c * c)):
                sums[n] = term if sums[n] is None else sums[n] + term
    stacked = dead
    for n in range(6):
        stacked = jnp.where(sub == n, jnp.sum(sums[n], axis=0, keepdims=True), stacked)
    stacked = jnp.where(sub == lane, jnp.sum(stacked, axis=1, keepdims=True), dead)
    red1[row_at] = jnp.sum(stacked, axis=0, keepdims=True)
    for p in row_peers:
        pltpu.make_async_remote_copy(
            src_ref=red1.at[row_at], dst_ref=red1.at[row_at], send_sem=red_send.at[0], recv_sem=red_recv.at[0], device_id=p,
            device_id_type=MESH,
        ).start()
    all_row = pltpu.make_async_remote_copy(
        src_ref=red1.at[pl.ds(0, ROW - 1)], dst_ref=red1.at[pl.ds(0, ROW - 1)], send_sem=red_send.at[0],
        recv_sem=red_recv.at[0], device_id=prv, device_id_type=MESH,
    )
    all_row.wait_recv()
    total = red1[0]
    for n in range(1, ROW):
        total = total + red1[n]
    red2[plane_at] = total
    for p in plane_peers:
        pltpu.make_async_remote_copy(
            src_ref=red2.at[plane_at], dst_ref=red2.at[plane_at], send_sem=red_send.at[1], recv_sem=red_recv.at[1],
            device_id=p, device_id_type=MESH,
        ).start()
    count = SECTIONS * COLS - 1
    all_plane = pltpu.make_async_remote_copy(
        src_ref=red2.at[pl.ds(0, count)], dst_ref=red2.at[pl.ds(0, count)], send_sem=red_send.at[1],
        recv_sem=red_recv.at[1], device_id=prv, device_id_type=MESH,
    )
    all_plane.wait_recv()
    one, two = [], []
    start = None
    for t in range(SECTIONS):
        total = red2[COLS * t]
        for n in range(1, COLS):
            total = total + red2[COLS * t + n]
        g = [jnp.sum(jnp.where(lane[0:1] == n, total, 0.0), axis=1, keepdims=True) for n in range(6)]
        ratio = g[4] / g[2]
        c2 = (g[3] - ratio * g[1]) / (g[5] - ratio * g[4])
        c1 = g[1] / g[2] - ratio * c2
        one.append(t_row[t] * c1)
        two.append(t_row[t] * c2)
        start = g[0] if start is None else jnp.where(s == t, g[0], start)
    rms[...] = jnp.broadcast_to(jnp.sqrt(start) / np.float32(np.sqrt(np.float32(VARS * NODES * LANES * 128))), rms.shape)
    for c in dir_copies:
        c.wait_recv()
    for k in range(VARS):
        for q in range(8):
            rows = pl.ds(8 * q, 8)
            total = None
            for t in range(SECTIONS):
                term = one[t] * dirs[0, t, k, rows, :] + two[t] * dirs[1, t, k, rows, :]
                total = term if total is None else total + term
            out[0, k, rows, :] = total
    for c in res_copies + dir_copies + halo_copies + [all_row, all_plane]:
        c.wait_send()


def local(*args):
    hbm = pl.BlockSpec(memory_space=pltpu.HBM)
    ANY = pl.BlockSpec(memory_space=pl.ANY)
    vmem = pl.BlockSpec(memory_space=pltpu.VMEM)
    dma = pltpu.SemaphoreType.DMA
    slopes = jnp.asarray(slope_matrix())
    args = list(args)
    args[3] = jnp.transpose(args[3], (1, 2, 0, 3))
    args[5] = jnp.transpose(args[5], (1, 2, 0, 3))
    update, rms = pl.pallas_call(
        body,
        out_shape=(
            pltpu.VMEM((1, VARS, NODES, LANES), F32),
            pltpu.VMEM((1, LANES), F32),
        ),
        in_specs=[hbm, hbm, ANY] + [hbm] * 6 + [ANY, hbm],
        out_specs=(vmem, vmem),
        scratch_shapes=[
            pltpu.VMEM((SECTIONS, VARS, NODES, LANES), F32),
            pltpu.VMEM((VARS, VARS, 3, LANES), F32),
            pltpu.VMEM((6, LANES), F32),
            pltpu.VMEM((VARS, VARS, 1, LANES), F32),
            pltpu.VMEM((NODES, NODES), F32),
            pltpu.VMEM((6, LANES), I32),
            pltpu.VMEM((6, LANES), I32),
            pltpu.VMEM((4 * NODES, NODES), F32),
            pltpu.SMEM((4, 4), F32),
            pltpu.SMEM((1,), F32),
            pltpu.SMEM((1,), I32),
            pltpu.VMEM((4 * NODES, NODES), F32),
            pltpu.VMEM((3, VARS, VARS, LANES), F32),
            pltpu.VMEM((VARS, VARS, LANES), F32),
            pltpu.VMEM((8, 8, LANES), F32),
            pltpu.VMEM((20, 8, LANES), F32),
            pltpu.VMEM((20, 8, LANES), I32),
            pltpu.VMEM((6, 8, LANES), I32),
            pltpu.VMEM((12, 8, LANES), I32),
            pltpu.VMEM((VARS, 4 * NODES, LANES), F32),
            pltpu.VMEM((VARS, NODES, LANES), F32),
            pltpu.VMEM((2, VARS, NODES, LANES), F32),
            pltpu.VMEM((2, SECTIONS, VARS, NODES, LANES), F32),
            pltpu.VMEM((60, 8, LANES), F32),
            pltpu.VMEM((60, 8, LANES), F32),
            pltpu.VMEM((2, 2, 15, 8, LANES), F32),
            pltpu.VMEM((2, 2, 15, 8, LANES), F32),
            pltpu.VMEM((ROW, 1, LANES), F32),
            pltpu.VMEM((SECTIONS * COLS, 1, LANES), F32),
            dma((11,)), dma((3,)), dma((3,)), dma((2, 3)), dma((2, 3)), dma((2, 2)), dma((2, 2)), dma((2,)), dma((2,)),
        ],
        compiler_params=pltpu.CompilerParams(collective_id=0, has_side_effects=True, vmem_limit_bytes=32 * 1024 * 1024),
        name="newton_step",
    )(*[x if x.shape == (1,) else pltpu.with_memory_space_constraint(x, pltpu.HBM) for x in args + [slopes]])
    return update, rms[0, 0:1]


def solution(mesh):
    placed = (
        P("section", None, None, "elem"), P(), P("section"), P(None, None, None, "elem"), P(None, "elem"),
        P("section", None, None, "elem"), P("section", None, None), P(None, "elem"), P(None, "elem"), P("elem"),
    )
    return jax.shard_map(
        local, mesh=mesh, in_specs=placed, out_specs=(P("section", None, None, "elem"), P("section")), check_vma=False,
    )
```

```python
import functools

import jax
import jax.numpy as jnp
import numpy as np
from jax import lax
from jax.experimental import pallas as pl
from jax.experimental.pallas import tpu as pltpu
from jax.sharding import PartitionSpec as P

MESH = pl.DeviceIdType.MESH
F32 = jnp.float32
I32 = jnp.int32
VARS, NODES, LANES, HALO = 5, 64, 128, 32
SECTIONS, ROW, COLS = 4, 16, 8


def derivative_table():
    points = np.array([-1.0, -np.sqrt(0.2), np.sqrt(0.2), 1.0])
    weights = np.array([1.0 / np.prod([points[b] - points[c] for c in range(4) if c != b]) for b in range(4)])
    table = np.zeros((4, 4))
    for a in range(4):
        for b in range(4):
            if a != b:
                table[a, b] = weights[b] / weights[a] / (points[a] - points[b])
        table[a, a] = -np.sum(table[a])
    return table


def slope_matrix():
    table, eye = derivative_table().astype(np.float32).astype(np.float64), np.eye(4)
    parts = [np.eye(NODES)]
    for spots in ((table, eye, eye), (eye, table, eye), (eye, eye, table)):
        parts.append(np.kron(np.kron(spots[0], spots[1]), spots[2]))
    return np.concatenate(parts).astype(np.float32)


def dot(a, b):
    return jnp.dot(a, b, precision=lax.Precision.HIGHEST, preferred_element_type=F32)


def inverse_of(entries):
    left = [[entries[i][j] for j in range(4)] for i in range(4)]
    right = [[jnp.full_like(entries[0][0], 1.0 if i == j else 0.0) for j in range(4)] for i in range(4)]
    for pivot in range(4):
        scale = 1.0 / left[pivot][pivot]
        left[pivot] = [x * scale for x in left[pivot]]
        right[pivot] = [x * scale for x in right[pivot]]
        for target in range(4):
            if target != pivot:
                factor = left[target][pivot]
                left[target] = [x - factor * y for x, y in zip(left[target], left[pivot])]
                right[target] = [x - factor * y for x, y in zip(right[target], right[pivot])]
    return right


def pick(choices, which):
    out = choices[0]
    for i in range(1, len(choices)):
        out = jnp.where(which == i, choices[i], out)
    return out


def face_rows(u):
    sub = lax.broadcasted_iota(I32, (8, LANES), 0)
    low = sub < 4
    rows = [[u[0][0], u[0][1]], [u[3][0], u[3][1]], [], [], [], []]
    for h in range(2):
        a, b = u[2 * h], u[2 * h + 1]
        rows[2].append(jnp.where(low, a[0], pltpu.roll(b[0], 4, 0)))
        rows[3].append(jnp.where(low, pltpu.roll(a[1], 4, 0), b[1]))
    for f, k in ((4, 0), (5, 3)):
        at = k + 4 * (sub & 1)
        for h in range(2):
            a, b = u[2 * h], u[2 * h + 1]
            s = [jnp.take_along_axis(x, at, axis=0) for x in (a[0], a[1], b[0], b[1])]
            rows[f].append(jnp.where(low, jnp.where(sub < 2, s[0], s[1]), jnp.where(sub < 6, s[2], s[3])))
    return rows


def turned(a, b, code):
    swap = (code & 4) != 0
    a2 = jnp.where(swap, b, a)
    b2 = jnp.where(swap, a, b)
    a2 = jnp.where((code & 1) != 0, 3 - a2, a2)
    b2 = jnp.where((code & 2) != 0, 3 - b2, b2)
    return 4 * a2 + b2


def body(
    residual, transform, shifts, flux, penalty, block_inverse, nodal_inverse, neighbours, orientation, live_counts, slopes,
    out, rms,
    v_res, v_flux, v_pen, v_block, v_nodal, v_neigh, v_orient, v_slopes, s_transform, s_shift, s_live,
    n_all, mixed, blocks, pen_node, far_coef, far_row, own_at, halo_at, y, r, w, dirs, faces, near, pack, halo, red1, red2,
    in_sem, res_send, res_recv, pass_send, pass_recv, dir_send, dir_recv, halo_send, halo_recv, red_send, red_recv,
):
    s, e = lax.axis_index("section"), lax.axis_index("elem")
    x_peers = [(lax.rem(s + k, SECTIONS), e) for k in (1, 3, 2)]
    nxt, prv = (s, lax.rem(e + 1, 128)), (s, lax.rem(e + 127, 128))
    row_base = (e // ROW) * ROW
    row_at = e - row_base
    row_peers = [(s, row_base + lax.rem(row_at + k, ROW)) for k in (8, 9, 7, 6, 10, 5, 11, 4, 12, 3, 13, 2, 14, 15, 1)]
    plane_at = s * COLS + e // ROW
    plane_peers = []
    for k in (2, 1, 3, 0):
        for q in (4, 3, 5, 2, 6, 1, 7, 0):
            if k or q:
                plane_peers.append((lax.rem(s + k, SECTIONS), lax.rem(e + ROW * q, 128)))

    barrier = pltpu.get_barrier_semaphore()
    peers = x_peers + [nxt, prv] + row_peers + plane_peers
    for p in peers:
        pl.semaphore_signal(barrier, inc=1, device_id=p, device_id_type=MESH)

    loads = [
        (residual.at[0], v_res.at[s]), (flux, v_flux), (penalty, v_pen), (block_inverse, v_block), (nodal_inverse.at[0], v_nodal),
        (neighbours, v_neigh), (orientation, v_orient), (slopes, v_slopes), (transform, s_transform), (shifts, s_shift),
        (live_counts, s_live),
    ]
    loads = [pltpu.make_async_copy(a, b, in_sem.at[i]) for i, (a, b) in enumerate(loads)]
    for c in loads:
        c.start()

    pl.semaphore_wait(barrier, len(peers))
    sides = x_peers[:2]
    behind = [lax.rem(s + 3, SECTIONS), lax.rem(s + 1, SECTIONS)]
    res_copies = [[None] * VARS for _ in range(2)]
    for n in range(VARS):
        for d in range(2):
            k = n if d == 0 else VARS - 1 - n
            c = pltpu.make_async_remote_copy(
                src_ref=residual.at[0, k], dst_ref=v_res.at[s, k], send_sem=res_send.at[d, k], recv_sem=res_recv.at[d, k],
                device_id=sides[d], device_id_type=MESH,
            )
            c.start()
            res_copies[d][k] = c
    for c in loads:
        c.wait()

    lane = lax.broadcasted_iota(I32, (8, LANES), 1)
    sub = lax.broadcasted_iota(I32, (8, LANES), 0)
    mask = jnp.where(lane < s_live[0], 1.0, 0.0).astype(F32)
    mask1 = mask[0:1]
    t_entries = [[jnp.full((8, LANES), s_transform[i, j], F32) for j in range(4)] for i in range(4)]
    inverse = inverse_of(t_entries)
    mix = [pick([inverse[i][t] for i in range(4)], s) * mask for t in range(4)]
    t_row = [pick([t_entries[i][t] for i in range(4)], s) for t in range(4)]

    n_full = dot(v_slopes[...], v_nodal[...])
    n_high = n_full.astype(jnp.bfloat16)
    n_all[0:4 * NODES, :] = n_high
    n_all[4 * NODES:8 * NODES, :] = (n_full - n_high.astype(F32)).astype(jnp.bfloat16)

    def spread(k, x):
        high = x.astype(jnp.bfloat16)
        low = (x - high.astype(F32)).astype(jnp.bfloat16)
        first = jnp.dot(n_all[...], high, preferred_element_type=F32)
        second = jnp.dot(n_all[0:4 * NODES, :], low, preferred_element_type=F32)
        y[k] = first[0:4 * NODES] + (first[4 * NODES:8 * NODES] + second)

    for m in range(VARS):
        blocks[m] = jnp.concatenate([v_block[m, c] for c in range(VARS)], axis=0) * mask1
    for d in range(3):
        for k in range(VARS):
            total = None
            for m in range(VARS):
                term = v_flux[k, m, d:d + 1, :] * blocks[m]
                total = term if total is None else total + term
            mixed[d, k] = total

    dead = jnp.zeros((8, LANES), F32)
    coef, code = [], []
    for f in range(6):
        far = jnp.broadcast_to(v_neigh[f:f + 1, :], (8, LANES))
        there = far >= 0
        at = far - e * LANES
        inside = there & (at >= 0) & (at < LANES)
        before = there & (at < 0)
        after = there & (at >= LANES)
        own_at[f] = jnp.where(inside, at, 0)
        halo_at[f] = jnp.where(before, at + HALO, jnp.where(after, at - LANES, 0))
        halo_at[6 + f] = jnp.where(before, 1, jnp.where(after, 2, 0))
        coef.append(jnp.where(there, jnp.broadcast_to(v_pen[f:f + 1, :], (8, LANES)), dead) * mask)
        code.append(jnp.broadcast_to(v_orient[f:f + 1, :], (8, LANES)))
    k_at, j_low = sub & 3, sub >> 2
    for n, (i, jh) in enumerate(((0, 0), (0, 1), (3, 0), (3, 1))):
        f = 0 if i == 0 else 1
        far_coef[n] = coef[f]
        far_row[n] = turned(2 * jh + j_low, k_at, code[f])
    for i in range(4):
        for jh in range(2):
            n = 4 + 2 * i + jh
            f = 2 + jh
            far_coef[n] = jnp.where(j_low == jh, coef[f], dead)
            far_row[n] = turned(jnp.full((8, LANES), i, I32), k_at, code[f])
            n += 8
            low_face = k_at < 2
            far_coef[n] = jnp.where(k_at == 0, coef[4], jnp.where(k_at == 3, coef[5], dead))
            far_row[n] = turned(jnp.full((8, LANES), i, I32), 2 * jh + j_low, jnp.where(low_face, code[4], code[5]))
    own_pen = [jnp.broadcast_to(v_pen[f:f + 1, :], (8, LANES)) for f in range(6)]
    for i in range(4):
        for jh in range(2):
            total = jnp.full((8, LANES), s_shift[0], F32)
            if i in (0, 3):
                total = total + own_pen[0 if i == 0 else 1]
            total = total + jnp.where(j_low == jh, own_pen[2 + jh], dead)
            total = total + jnp.where(k_at == 0, own_pen[4], jnp.where(k_at == 3, own_pen[5], dead))
            pen_node[2 * i + jh] = total

    passed = [[], []]
    for n in range(3):
        for d in range(2):
            k = n if d == 0 else VARS - 1 - n
            res_copies[d][k].wait_recv()
            rows = pl.ds(0, NODES) if n < 2 else pl.ds(NODES // 2 * d, NODES // 2)
            part = v_res.at[behind[d], k, rows]
            c = pltpu.make_async_remote_copy(
                src_ref=part, dst_ref=part, send_sem=pass_send.at[d, n], recv_sem=pass_recv.at[d, n], device_id=sides[d],
                device_id_type=MESH,
            )
            c.start()
            passed[d].append(c)
    for k in (0, 4, 1, 3, 2):
        if k < 2:
            res_copies[1][k].wait_recv()
            passed[0][k].wait_recv()
        elif k > 2:
            res_copies[0][k].wait_recv()
            passed[1][VARS - 1 - k].wait_recv()
        else:
            passed[0][2].wait_recv()
            passed[1][2].wait_recv()
        for q in range(8):
            rows = pl.ds(8 * q, 8)
            total = mix[0] * v_res[0, k, rows, :]
            for t in range(1, 4):
                total = total + mix[t] * v_res[t, k, rows, :]
            r[k, rows, :] = total
        spread(k, r[k])

    dir_copies, halo_copies = [], []

    def operator(step, target):
        for k in range(VARS):
            total = None
            for c in range(VARS):
                term = blocks[k, c:c + 1, :] * y[c, 0:NODES, :]
                total = term if total is None else total + term
            dirs[step, s, k] = total
        for k in range(VARS):
            u = [[dirs[step, s, k, pl.ds(16 * i + 8 * jh, 8), :] for jh in range(2)] for i in range(4)]
            rows = face_rows(u)
            for f in range(6):
                for h in range(2):
                    faces[f * 10 + k * 2 + h] = rows[f][h]
        group = lane >> 5
        for p in range(15):
            x = [faces[4 * p + g] for g in range(4)]
            x = [x[0]] + [pltpu.roll(x[g], 32 * g, 1) for g in range(1, 4)]
            pack[step, 0, p] = jnp.where(group < 2, jnp.where(group == 0, x[0], x[1]), jnp.where(group == 2, x[2], x[3]))
            pack[step, 1, p] = jnp.where(group < 2, jnp.where(group == 0, x[1], x[2]), jnp.where(group == 2, x[3], x[0]))
        waits = []
        for side, p in ((0, prv), (1, nxt)):
            c = pltpu.make_async_remote_copy(
                src_ref=pack.at[step, side], dst_ref=halo.at[step, side], send_sem=halo_send.at[step, side],
                recv_sem=halo_recv.at[step, side], device_id=p, device_id_type=MESH,
            )
            c.start()
            waits.append(c)
            halo_copies.append(c)
        for j, p in enumerate(x_peers):
            c = pltpu.make_async_remote_copy(
                src_ref=dirs.at[step, s], dst_ref=dirs.at[step, s], send_sem=dir_send.at[step, j],
                recv_sem=dir_recv.at[step, j], device_id=p, device_id_type=MESH,
            )
            c.start()
            dir_copies.append(c)
        for k in range(VARS):
            total = jnp.concatenate([pen_node[q] for q in range(8)], axis=0) * dirs[step, s, k]
            for d in range(3):
                for c in range(VARS):
                    total = total + mixed[d, k, c:c + 1, :] * y[c, NODES * (d + 1):NODES * (d + 2), :]
            target[k] = total
        for f in range(6):
            at = own_at[f]
            for n in range(10):
                near[f * 10 + n] = jnp.take_along_axis(faces[(f ^ 1) * 10 + n], at, axis=1)
        for c in waits:
            c.wait_recv()
        for f in range(6):
            at = halo_at[f]
            side = halo_at[6 + f]
            for n in range(10):
                m = (f ^ 1) * 10 + n
                p, g = m // 4, m % 4
                after = jnp.take_along_axis(halo[step, 0, p], at + 32 * g, axis=1)
                before = jnp.take_along_axis(halo[step, 1, p], at + 32 * ((g + 3) % 4), axis=1)
                near[f * 10 + n] = jnp.where(side == 0, near[f * 10 + n], jnp.where(side == 1, before, after))
        for n in range(20):
            row = far_row[n]
            at, high = row & 7, row >= 8
            if n < 4:
                f, i, jh = n // 2, 3 * (n // 2), n % 2
            else:
                i, jh = ((n - 4) % 8) // 2, n % 2
                f = 2 + jh if n < 12 else 4
            for k in range(VARS):
                def turn(face):
                    a = jnp.take_along_axis(near[face * 10 + 2 * k], at, axis=0)
                    b = jnp.take_along_axis(near[face * 10 + 2 * k + 1], at, axis=0)
                    return jnp.where(high, b, a)

                far = turn(f) if f < 4 else jnp.where(k_at < 2, turn(4), turn(5))
                rows = pl.ds(16 * i + 8 * jh, 8)
                target[k, rows, :] = target[k, rows, :] - far_coef[n] * far

    operator(0, w.at[0])
    for k in range(VARS):
        spread(k, w[0, k])
    operator(1, w.at[1])

    sums = [None] * 6
    for k in range(VARS):
        for q in range(8):
            rows = pl.ds(8 * q, 8)
            a, b, c = r[k, rows, :], w[0, k, rows, :], w[1, k, rows, :]
            for n, term in enumerate((a * a, a * b, b * b, a * c, b * c, c * c)):
                sums[n] = term if sums[n] is None else sums[n] + term
    stacked = dead
    for n in range(6):
        stacked = jnp.where(sub == n, jnp.sum(sums[n], axis=0, keepdims=True), stacked)
    stacked = jnp.where(sub == lane, jnp.sum(stacked, axis=1, keepdims=True), dead)
    red1[row_at] = jnp.sum(stacked, axis=0, keepdims=True)
    for p in row_peers:
        pltpu.make_async_remote_copy(
            src_ref=red1.at[row_at], dst_ref=red1.at[row_at], send_sem=red_send.at[0], recv_sem=red_recv.at[0], device_id=p,
            device_id_type=MESH,
        ).start()
    all_row = pltpu.make_async_remote_copy(
        src_ref=red1.at[pl.ds(0, ROW - 1)], dst_ref=red1.at[pl.ds(0, ROW - 1)], send_sem=red_send.at[0],
        recv_sem=red_recv.at[0], device_id=prv, device_id_type=MESH,
    )
    all_row.wait_recv()
    total = red1[0]
    for n in range(1, ROW):
        total = total + red1[n]
    red2[plane_at] = total
    for p in plane_peers:
        pltpu.make_async_remote_copy(
            src_ref=red2.at[plane_at], dst_ref=red2.at[plane_at], send_sem=red_send.at[1], recv_sem=red_recv.at[1],
            device_id=p, device_id_type=MESH,
        ).start()
    count = SECTIONS * COLS - 1
    all_plane = pltpu.make_async_remote_copy(
        src_ref=red2.at[pl.ds(0, count)], dst_ref=red2.at[pl.ds(0, count)], send_sem=red_send.at[1],
        recv_sem=red_recv.at[1], device_id=prv, device_id_type=MESH,
    )
    all_plane.wait_recv()
    one, two = [], []
    start = None
    for t in range(SECTIONS):
        total = red2[COLS * t]
        for n in range(1, COLS):
            total = total + red2[COLS * t + n]
        g = [jnp.sum(jnp.where(lane[0:1] == n, total, 0.0), axis=1, keepdims=True) for n in range(6)]
        ratio = g[4] / g[2]
        c2 = (g[3] - ratio * g[1]) / (g[5] - ratio * g[4])
        c1 = g[1] / g[2] - ratio * c2
        one.append(t_row[t] * c1)
        two.append(t_row[t] * c2)
        start = g[0] if start is None else jnp.where(s == t, g[0], start)
    rms[...] = jnp.broadcast_to(jnp.sqrt(start) / np.float32(np.sqrt(np.float32(VARS * NODES * LANES * 128))), rms.shape)
    for c in dir_copies:
        c.wait_recv()
    for k in range(VARS):
        for q in range(8):
            rows = pl.ds(8 * q, 8)
            total = None
            for t in range(SECTIONS):
                term = one[t] * dirs[0, t, k, rows, :] + two[t] * dirs[1, t, k, rows, :]
                total = term if total is None else total + term
            out[0, k, rows, :] = total
    for c in res_copies[0] + res_copies[1] + passed[0] + passed[1] + dir_copies + halo_copies + [all_row, all_plane]:
        c.wait_send()


def local(*args):
    hbm = pl.BlockSpec(memory_space=pltpu.HBM)
    ANY = pl.BlockSpec(memory_space=pl.ANY)
    vmem = pl.BlockSpec(memory_space=pltpu.VMEM)
    dma = pltpu.SemaphoreType.DMA
    slopes = jnp.asarray(slope_matrix())
    args = list(args)
    args[3] = jnp.transpose(args[3], (1, 2, 0, 3))
    args[5] = jnp.transpose(args[5], (1, 2, 0, 3))
    update, rms = pl.pallas_call(
        body,
        out_shape=(
            pltpu.VMEM((1, VARS, NODES, LANES), F32),
            pltpu.VMEM((1, LANES), F32),
        ),
        in_specs=[hbm, hbm, ANY] + [hbm] * 6 + [ANY, hbm],
        out_specs=(vmem, vmem),
        scratch_shapes=[
            pltpu.VMEM((SECTIONS, VARS, NODES, LANES), F32),
            pltpu.VMEM((VARS, VARS, 3, LANES), F32),
            pltpu.VMEM((6, LANES), F32),
            pltpu.VMEM((VARS, VARS, 1, LANES), F32),
            pltpu.VMEM((NODES, NODES), F32),
            pltpu.VMEM((6, LANES), I32),
            pltpu.VMEM((6, LANES), I32),
            pltpu.VMEM((4 * NODES, NODES), F32),
            pltpu.SMEM((4, 4), F32),
            pltpu.SMEM((1,), F32),
            pltpu.SMEM((1,), I32),
            pltpu.VMEM((8 * NODES, NODES), jnp.bfloat16),
            pltpu.VMEM((3, VARS, VARS, LANES), F32),
            pltpu.VMEM((VARS, VARS, LANES), F32),
            pltpu.VMEM((8, 8, LANES), F32),
            pltpu.VMEM((20, 8, LANES), F32),
            pltpu.VMEM((20, 8, LANES), I32),
            pltpu.VMEM((6, 8, LANES), I32),
            pltpu.VMEM((12, 8, LANES), I32),
            pltpu.VMEM((VARS, 4 * NODES, LANES), F32),
            pltpu.VMEM((VARS, NODES, LANES), F32),
            pltpu.VMEM((2, VARS, NODES, LANES), F32),
            pltpu.VMEM((2, SECTIONS, VARS, NODES, LANES), F32),
            pltpu.VMEM((60, 8, LANES), F32),
            pltpu.VMEM((60, 8, LANES), F32),
            pltpu.VMEM((2, 2, 15, 8, LANES), F32),
            pltpu.VMEM((2, 2, 15, 8, LANES), F32),
            pltpu.VMEM((ROW, 1, LANES), F32),
            pltpu.VMEM((SECTIONS * COLS, 1, LANES), F32),
            dma((11,)), dma((2, VARS)), dma((2, VARS)), dma((2, 3)), dma((2, 3)), dma((2, 3)), dma((2, 3)), dma((2, 2)), dma((2, 2)), dma((2,)), dma((2,)),
        ],
        compiler_params=pltpu.CompilerParams(collective_id=0, has_side_effects=True, vmem_limit_bytes=32 * 1024 * 1024),
        name="newton_step",
    )(*[x if x.shape == (1,) else pltpu.with_memory_space_constraint(x, pltpu.HBM) for x in args + [slopes]])
    return update, rms[0, 0:1]


def solution(mesh):
    placed = (
        P("section", None, None, "elem"), P(), P("section"), P(None, None, None, "elem"), P(None, "elem"),
        P("section", None, None, "elem"), P("section", None, None), P(None, "elem"), P(None, "elem"), P("elem"),
    )
    return jax.shard_map(
        local, mesh=mesh, in_specs=placed, out_specs=(P("section", None, None, "elem"), P("section")), check_vma=False,
    )
```

```python
import functools

import jax
import jax.numpy as jnp
import numpy as np
from jax import lax
from jax.experimental import pallas as pl
from jax.experimental.pallas import tpu as pltpu
from jax.sharding import PartitionSpec as P

MESH = pl.DeviceIdType.MESH
F32 = jnp.float32
I32 = jnp.int32
VARS, NODES, LANES, HALO = 5, 64, 128, 32
SECTIONS, ROW, COLS = 4, 16, 8


def derivative_table():
    points = np.array([-1.0, -np.sqrt(0.2), np.sqrt(0.2), 1.0])
    weights = np.array([1.0 / np.prod([points[b] - points[c] for c in range(4) if c != b]) for b in range(4)])
    table = np.zeros((4, 4))
    for a in range(4):
        for b in range(4):
            if a != b:
                table[a, b] = weights[b] / weights[a] / (points[a] - points[b])
        table[a, a] = -np.sum(table[a])
    return table


def slope_matrix():
    table, eye = derivative_table().astype(np.float32).astype(np.float64), np.eye(4)
    parts = [np.eye(NODES)]
    for spots in ((table, eye, eye), (eye, table, eye), (eye, eye, table)):
        parts.append(np.kron(np.kron(spots[0], spots[1]), spots[2]))
    return np.concatenate(parts).astype(np.float32)


def dot(a, b):
    return jnp.dot(a, b, precision=lax.Precision.HIGHEST, preferred_element_type=F32)


def inverse_of(entries):
    left = [[entries[i][j] for j in range(4)] for i in range(4)]
    right = [[jnp.full_like(entries[0][0], 1.0 if i == j else 0.0) for j in range(4)] for i in range(4)]
    for pivot in range(4):
        scale = 1.0 / left[pivot][pivot]
        left[pivot] = [x * scale for x in left[pivot]]
        right[pivot] = [x * scale for x in right[pivot]]
        for target in range(4):
            if target != pivot:
                factor = left[target][pivot]
                left[target] = [x - factor * y for x, y in zip(left[target], left[pivot])]
                right[target] = [x - factor * y for x, y in zip(right[target], right[pivot])]
    return right


def pick(choices, which):
    out = choices[0]
    for i in range(1, len(choices)):
        out = jnp.where(which == i, choices[i], out)
    return out


def face_rows(u):
    sub = lax.broadcasted_iota(I32, (8, LANES), 0)
    low = sub < 4
    rows = [[u[0][0], u[0][1]], [u[3][0], u[3][1]], [], [], [], []]
    for h in range(2):
        a, b = u[2 * h], u[2 * h + 1]
        rows[2].append(jnp.where(low, a[0], pltpu.roll(b[0], 4, 0)))
        rows[3].append(jnp.where(low, pltpu.roll(a[1], 4, 0), b[1]))
    for f, k in ((4, 0), (5, 3)):
        at = k + 4 * (sub & 1)
        for h in range(2):
            a, b = u[2 * h], u[2 * h + 1]
            s = [jnp.take_along_axis(x, at, axis=0) for x in (a[0], a[1], b[0], b[1])]
            rows[f].append(jnp.where(low, jnp.where(sub < 2, s[0], s[1]), jnp.where(sub < 6, s[2], s[3])))
    return rows


def turned(a, b, code):
    swap = (code & 4) != 0
    a2 = jnp.where(swap, b, a)
    b2 = jnp.where(swap, a, b)
    a2 = jnp.where((code & 1) != 0, 3 - a2, a2)
    b2 = jnp.where((code & 2) != 0, 3 - b2, b2)
    return 4 * a2 + b2


def body(
    residual, transform, shifts, flux, penalty, block_inverse, nodal_inverse, neighbours, orientation, live_counts, slopes,
    out, rms,
    v_res, v_flux, v_pen, v_block, v_nodal, v_neigh, v_orient, v_slopes, s_transform, s_shift, s_live,
    n_all, mixed, blocks, pen_node, far_coef, far_row, own_at, halo_at, y, r, w, dirs, faces, near, pack, halo, red1, red2,
    in_sem, res_send, res_recv, pass_send, pass_recv, dir_send, dir_recv, across_send, across_recv, halo_send, halo_recv, red_send, red_recv,
):
    s, e = lax.axis_index("section"), lax.axis_index("elem")
    x_peers = [(lax.rem(s + k, SECTIONS), e) for k in (1, 3, 2)]
    nxt, prv = (s, lax.rem(e + 1, 128)), (s, lax.rem(e + 127, 128))
    row_base = (e // ROW) * ROW
    row_at = e - row_base
    row_peers = [(s, row_base + lax.rem(row_at + k, ROW)) for k in (8, 9, 7, 6, 10, 5, 11, 4, 12, 3, 13, 2, 14, 15, 1)]
    plane_at = s * COLS + e // ROW
    plane_peers = []
    for k in (2, 1, 3, 0):
        for q in (4, 3, 5, 2, 6, 1, 7, 0):
            if k or q:
                plane_peers.append((lax.rem(s + k, SECTIONS), lax.rem(e + ROW * q, 128)))

    barrier = pltpu.get_barrier_semaphore()
    peers = x_peers + [nxt, prv] + row_peers + plane_peers
    for p in peers:
        pl.semaphore_signal(barrier, inc=1, device_id=p, device_id_type=MESH)

    loads = [
        (residual.at[0], v_res.at[s]), (flux, v_flux), (penalty, v_pen), (block_inverse, v_block), (nodal_inverse.at[0], v_nodal),
        (neighbours, v_neigh), (orientation, v_orient), (slopes, v_slopes), (transform, s_transform), (shifts, s_shift),
        (live_counts, s_live),
    ]
    loads = [pltpu.make_async_copy(a, b, in_sem.at[i]) for i, (a, b) in enumerate(loads)]
    for c in loads:
        c.start()

    pl.semaphore_wait(barrier, len(peers))
    sides = x_peers[:2]
    behind = [lax.rem(s + 3, SECTIONS), lax.rem(s + 1, SECTIONS)]
    res_copies = [[None] * VARS for _ in range(2)]
    for n in range(VARS):
        for d in range(2):
            k = n if d == 0 else VARS - 1 - n
            c = pltpu.make_async_remote_copy(
                src_ref=residual.at[0, k], dst_ref=v_res.at[s, k], send_sem=res_send.at[d, k], recv_sem=res_recv.at[d, k],
                device_id=sides[d], device_id_type=MESH,
            )
            c.start()
            res_copies[d][k] = c
    for c in loads:
        c.wait()

    lane = lax.broadcasted_iota(I32, (8, LANES), 1)
    sub = lax.broadcasted_iota(I32, (8, LANES), 0)
    mask = jnp.where(lane < s_live[0], 1.0, 0.0).astype(F32)
    mask1 = mask[0:1]
    t_entries = [[jnp.full((8, LANES), s_transform[i, j], F32) for j in range(4)] for i in range(4)]
    inverse = inverse_of(t_entries)
    mix = [pick([inverse[i][t] for i in range(4)], s) * mask for t in range(4)]
    t_row = [pick([t_entries[i][t] for i in range(4)], s) for t in range(4)]

    n_full = dot(v_slopes[...], v_nodal[...])
    n_high = n_full.astype(jnp.bfloat16)
    n_all[0:4 * NODES, :] = n_high
    n_all[4 * NODES:8 * NODES, :] = (n_full - n_high.astype(F32)).astype(jnp.bfloat16)

    def spread(k, x):
        high = x.astype(jnp.bfloat16)
        low = (x - high.astype(F32)).astype(jnp.bfloat16)
        first = jnp.dot(n_all[...], high, preferred_element_type=F32)
        second = jnp.dot(n_all[0:4 * NODES, :], low, preferred_element_type=F32)
        y[k] = first[0:4 * NODES] + (first[4 * NODES:8 * NODES] + second)

    for m in range(VARS):
        blocks[m] = jnp.concatenate([v_block[m, c] for c in range(VARS)], axis=0) * mask1
    for d in range(3):
        for k in range(VARS):
            total = None
            for m in range(VARS):
                term = v_flux[k, m, d:d + 1, :] * blocks[m]
                total = term if total is None else total + term
            mixed[d, k] = total

    dead = jnp.zeros((8, LANES), F32)
    coef, code = [], []
    for f in range(6):
        far = jnp.broadcast_to(v_neigh[f:f + 1, :], (8, LANES))
        there = far >= 0
        at = far - e * LANES
        inside = there & (at >= 0) & (at < LANES)
        before = there & (at < 0)
        after = there & (at >= LANES)
        own_at[f] = jnp.where(inside, at, 0)
        halo_at[f] = jnp.where(before, at + HALO, jnp.where(after, at - LANES, 0))
        halo_at[6 + f] = jnp.where(before, 1, jnp.where(after, 2, 0))
        coef.append(jnp.where(there, jnp.broadcast_to(v_pen[f:f + 1, :], (8, LANES)), dead) * mask)
        code.append(jnp.broadcast_to(v_orient[f:f + 1, :], (8, LANES)))
    k_at, j_low = sub & 3, sub >> 2
    for n, (i, jh) in enumerate(((0, 0), (0, 1), (3, 0), (3, 1))):
        f = 0 if i == 0 else 1
        far_coef[n] = coef[f]
        far_row[n] = turned(2 * jh + j_low, k_at, code[f])
    for i in range(4):
        for jh in range(2):
            n = 4 + 2 * i + jh
            f = 2 + jh
            far_coef[n] = jnp.where(j_low == jh, coef[f], dead)
            far_row[n] = turned(jnp.full((8, LANES), i, I32), k_at, code[f])
            n += 8
            low_face = k_at < 2
            far_coef[n] = jnp.where(k_at == 0, coef[4], jnp.where(k_at == 3, coef[5], dead))
            far_row[n] = turned(jnp.full((8, LANES), i, I32), 2 * jh + j_low, jnp.where(low_face, code[4], code[5]))
    own_pen = [jnp.broadcast_to(v_pen[f:f + 1, :], (8, LANES)) for f in range(6)]
    for i in range(4):
        for jh in range(2):
            total = jnp.full((8, LANES), s_shift[0], F32)
            if i in (0, 3):
                total = total + own_pen[0 if i == 0 else 1]
            total = total + jnp.where(j_low == jh, own_pen[2 + jh], dead)
            total = total + jnp.where(k_at == 0, own_pen[4], jnp.where(k_at == 3, own_pen[5], dead))
            pen_node[2 * i + jh] = total

    passed = [[], []]
    for n in range(3):
        for d in range(2):
            k = n if d == 0 else VARS - 1 - n
            res_copies[d][k].wait_recv()
            rows = pl.ds(0, NODES) if n < 2 else pl.ds(NODES // 2 * d, NODES // 2)
            part = v_res.at[behind[d], k, rows]
            c = pltpu.make_async_remote_copy(
                src_ref=part, dst_ref=part, send_sem=pass_send.at[d, n], recv_sem=pass_recv.at[d, n], device_id=sides[d],
                device_id_type=MESH,
            )
            c.start()
            passed[d].append(c)
    for k in (0, 4, 1, 3, 2):
        if k < 2:
            res_copies[1][k].wait_recv()
            passed[0][k].wait_recv()
        elif k > 2:
            res_copies[0][k].wait_recv()
            passed[1][VARS - 1 - k].wait_recv()
        else:
            passed[0][2].wait_recv()
            passed[1][2].wait_recv()
        for q in range(8):
            rows = pl.ds(8 * q, 8)
            total = mix[0] * v_res[0, k, rows, :]
            for t in range(1, 4):
                total = total + mix[t] * v_res[t, k, rows, :]
            r[k, rows, :] = total
        spread(k, r[k])

    dir_copies, across_copies, halo_copies = [], [], []

    def pass_on(step):
        for d in range(2):
            dir_copies[2 * step + d].wait_recv()
            part = dirs.at[step, behind[d], pl.ds(0, VARS), pl.ds(NODES // 2 * d, NODES // 2)]
            c = pltpu.make_async_remote_copy(
                src_ref=part, dst_ref=part, send_sem=across_send.at[step, d], recv_sem=across_recv.at[step, d],
                device_id=sides[d], device_id_type=MESH,
            )
            c.start()
            across_copies.append(c)

    def operator(step, target):
        for k in range(VARS):
            total = None
            for c in range(VARS):
                term = blocks[k, c:c + 1, :] * y[c, 0:NODES, :]
                total = term if total is None else total + term
            dirs[step, s, k] = total
        for k in range(VARS):
            u = [[dirs[step, s, k, pl.ds(16 * i + 8 * jh, 8), :] for jh in range(2)] for i in range(4)]
            rows = face_rows(u)
            for f in range(6):
                for h in range(2):
                    faces[f * 10 + k * 2 + h] = rows[f][h]
        group = lane >> 5
        for p in range(15):
            x = [faces[4 * p + g] for g in range(4)]
            x = [x[0]] + [pltpu.roll(x[g], 32 * g, 1) for g in range(1, 4)]
            pack[step, 0, p] = jnp.where(group < 2, jnp.where(group == 0, x[0], x[1]), jnp.where(group == 2, x[2], x[3]))
            pack[step, 1, p] = jnp.where(group < 2, jnp.where(group == 0, x[1], x[2]), jnp.where(group == 2, x[3], x[0]))
        waits = []
        for side, p in ((0, prv), (1, nxt)):
            c = pltpu.make_async_remote_copy(
                src_ref=pack.at[step, side], dst_ref=halo.at[step, side], send_sem=halo_send.at[step, side],
                recv_sem=halo_recv.at[step, side], device_id=p, device_id_type=MESH,
            )
            c.start()
            waits.append(c)
            halo_copies.append(c)
        for d in range(2):
            c = pltpu.make_async_remote_copy(
                src_ref=dirs.at[step, s], dst_ref=dirs.at[step, s], send_sem=dir_send.at[step, d],
                recv_sem=dir_recv.at[step, d], device_id=sides[d], device_id_type=MESH,
            )
            c.start()
            dir_copies.append(c)
        if step == 1:
            pass_on(0)
        for k in range(VARS):
            total = jnp.concatenate([pen_node[q] for q in range(8)], axis=0) * dirs[step, s, k]
            for d in range(3):
                for c in range(VARS):
                    total = total + mixed[d, k, c:c + 1, :] * y[c, NODES * (d + 1):NODES * (d + 2), :]
            target[k] = total
        for f in range(6):
            at = own_at[f]
            for n in range(10):
                near[f * 10 + n] = jnp.take_along_axis(faces[(f ^ 1) * 10 + n], at, axis=1)
        for c in waits:
            c.wait_recv()
        for f in range(6):
            at = halo_at[f]
            side = halo_at[6 + f]
            for n in range(10):
                m = (f ^ 1) * 10 + n
                p, g = m // 4, m % 4
                after = jnp.take_along_axis(halo[step, 0, p], at + 32 * g, axis=1)
                before = jnp.take_along_axis(halo[step, 1, p], at + 32 * ((g + 3) % 4), axis=1)
                near[f * 10 + n] = jnp.where(side == 0, near[f * 10 + n], jnp.where(side == 1, before, after))
        for n in range(20):
            row = far_row[n]
            at, high = row & 7, row >= 8
            if n < 4:
                f, i, jh = n // 2, 3 * (n // 2), n % 2
            else:
                i, jh = ((n - 4) % 8) // 2, n % 2
                f = 2 + jh if n < 12 else 4
            for k in range(VARS):
                def turn(face):
                    a = jnp.take_along_axis(near[face * 10 + 2 * k], at, axis=0)
                    b = jnp.take_along_axis(near[face * 10 + 2 * k + 1], at, axis=0)
                    return jnp.where(high, b, a)

                far = turn(f) if f < 4 else jnp.where(k_at < 2, turn(4), turn(5))
                rows = pl.ds(16 * i + 8 * jh, 8)
                target[k, rows, :] = target[k, rows, :] - far_coef[n] * far

    operator(0, w.at[0])
    for k in range(VARS):
        spread(k, w[0, k])
    operator(1, w.at[1])

    sums = [None] * 6
    for k in range(VARS):
        for q in range(8):
            rows = pl.ds(8 * q, 8)
            a, b, c = r[k, rows, :], w[0, k, rows, :], w[1, k, rows, :]
            for n, term in enumerate((a * a, a * b, b * b, a * c, b * c, c * c)):
                sums[n] = term if sums[n] is None else sums[n] + term
    stacked = dead
    for n in range(6):
        stacked = jnp.where(sub == n, jnp.sum(sums[n], axis=0, keepdims=True), stacked)
    stacked = jnp.where(sub == lane, jnp.sum(stacked, axis=1, keepdims=True), dead)
    red1[row_at] = jnp.sum(stacked, axis=0, keepdims=True)
    for p in row_peers:
        pltpu.make_async_remote_copy(
            src_ref=red1.at[row_at], dst_ref=red1.at[row_at], send_sem=red_send.at[0], recv_sem=red_recv.at[0], device_id=p,
            device_id_type=MESH,
        ).start()
    all_row = pltpu.make_async_remote_copy(
        src_ref=red1.at[pl.ds(0, ROW - 1)], dst_ref=red1.at[pl.ds(0, ROW - 1)], send_sem=red_send.at[0],
        recv_sem=red_recv.at[0], device_id=prv, device_id_type=MESH,
    )
    pass_on(1)
    all_row.wait_recv()
    total = red1[0]
    for n in range(1, ROW):
        total = total + red1[n]
    red2[plane_at] = total
    for p in plane_peers:
        pltpu.make_async_remote_copy(
            src_ref=red2.at[plane_at], dst_ref=red2.at[plane_at], send_sem=red_send.at[1], recv_sem=red_recv.at[1],
            device_id=p, device_id_type=MESH,
        ).start()
    count = SECTIONS * COLS - 1
    all_plane = pltpu.make_async_remote_copy(
        src_ref=red2.at[pl.ds(0, count)], dst_ref=red2.at[pl.ds(0, count)], send_sem=red_send.at[1],
        recv_sem=red_recv.at[1], device_id=prv, device_id_type=MESH,
    )
    all_plane.wait_recv()
    one, two = [], []
    start = None
    for t in range(SECTIONS):
        total = red2[COLS * t]
        for n in range(1, COLS):
            total = total + red2[COLS * t + n]
        g = [jnp.sum(jnp.where(lane[0:1] == n, total, 0.0), axis=1, keepdims=True) for n in range(6)]
        ratio = g[4] / g[2]
        c2 = (g[3] - ratio * g[1]) / (g[5] - ratio * g[4])
        c1 = g[1] / g[2] - ratio * c2
        one.append(t_row[t] * c1)
        two.append(t_row[t] * c2)
        start = g[0] if start is None else jnp.where(s == t, g[0], start)
    rms[...] = jnp.broadcast_to(jnp.sqrt(start) / np.float32(np.sqrt(np.float32(VARS * NODES * LANES * 128))), rms.shape)
    for c in across_copies:
        c.wait_recv()
    for k in range(VARS):
        for q in range(8):
            rows = pl.ds(8 * q, 8)
            total = None
            for t in range(SECTIONS):
                term = one[t] * dirs[0, t, k, rows, :] + two[t] * dirs[1, t, k, rows, :]
                total = term if total is None else total + term
            out[0, k, rows, :] = total
    for c in res_copies[0] + res_copies[1] + passed[0] + passed[1] + dir_copies + across_copies + halo_copies + [all_row, all_plane]:
        c.wait_send()


def local(*args):
    hbm = pl.BlockSpec(memory_space=pltpu.HBM)
    ANY = pl.BlockSpec(memory_space=pl.ANY)
    vmem = pl.BlockSpec(memory_space=pltpu.VMEM)
    dma = pltpu.SemaphoreType.DMA
    slopes = jnp.asarray(slope_matrix())
    args = list(args)
    args[3] = jnp.transpose(args[3], (1, 2, 0, 3))
    args[5] = jnp.transpose(args[5], (1, 2, 0, 3))
    update, rms = pl.pallas_call(
        body,
        out_shape=(
            pltpu.VMEM((1, VARS, NODES, LANES), F32),
            pltpu.VMEM((1, LANES), F32),
        ),
        in_specs=[hbm, hbm, ANY] + [hbm] * 6 + [ANY, hbm],
        out_specs=(vmem, vmem),
        scratch_shapes=[
            pltpu.VMEM((SECTIONS, VARS, NODES, LANES), F32),
            pltpu.VMEM((VARS, VARS, 3, LANES), F32),
            pltpu.VMEM((6, LANES), F32),
            pltpu.VMEM((VARS, VARS, 1, LANES), F32),
            pltpu.VMEM((NODES, NODES), F32),
            pltpu.VMEM((6, LANES), I32),
            pltpu.VMEM((6, LANES), I32),
            pltpu.VMEM((4 * NODES, NODES), F32),
            pltpu.SMEM((4, 4), F32),
            pltpu.SMEM((1,), F32),
            pltpu.SMEM((1,), I32),
            pltpu.VMEM((8 * NODES, NODES), jnp.bfloat16),
            pltpu.VMEM((3, VARS, VARS, LANES), F32),
            pltpu.VMEM((VARS, VARS, LANES), F32),
            pltpu.VMEM((8, 8, LANES), F32),
            pltpu.VMEM((20, 8, LANES), F32),
            pltpu.VMEM((20, 8, LANES), I32),
            pltpu.VMEM((6, 8, LANES), I32),
            pltpu.VMEM((12, 8, LANES), I32),
            pltpu.VMEM((VARS, 4 * NODES, LANES), F32),
            pltpu.VMEM((VARS, NODES, LANES), F32),
            pltpu.VMEM((2, VARS, NODES, LANES), F32),
            pltpu.VMEM((2, SECTIONS, VARS, NODES, LANES), F32),
            pltpu.VMEM((60, 8, LANES), F32),
            pltpu.VMEM((60, 8, LANES), F32),
            pltpu.VMEM((2, 2, 15, 8, LANES), F32),
            pltpu.VMEM((2, 2, 15, 8, LANES), F32),
            pltpu.VMEM((ROW, 1, LANES), F32),
            pltpu.VMEM((SECTIONS * COLS, 1, LANES), F32),
            dma((11,)), dma((2, VARS)), dma((2, VARS)), dma((2, 3)), dma((2, 3)), dma((2, 2)), dma((2, 2)), dma((2, 2)), dma((2, 2)),
            dma((2, 2)), dma((2, 2)), dma((2,)), dma((2,)),
        ],
        compiler_params=pltpu.CompilerParams(collective_id=0, has_side_effects=True, vmem_limit_bytes=32 * 1024 * 1024),
        name="newton_step",
    )(*[x if x.shape == (1,) else pltpu.with_memory_space_constraint(x, pltpu.HBM) for x in args + [slopes]])
    return update, rms[0, 0:1]


def solution(mesh):
    placed = (
        P("section", None, None, "elem"), P(), P("section"), P(None, None, None, "elem"), P(None, "elem"),
        P("section", None, None, "elem"), P("section", None, None), P(None, "elem"), P(None, "elem"), P("elem"),
    )
    return jax.shard_map(
        local, mesh=mesh, in_specs=placed, out_specs=(P("section", None, None, "elem"), P("section")), check_vma=False,
    )
```

```python
import functools

import jax
import jax.numpy as jnp
import numpy as np
from jax import lax
from jax.experimental import pallas as pl
from jax.experimental.pallas import tpu as pltpu
from jax.sharding import PartitionSpec as P

MESH = pl.DeviceIdType.MESH
F32 = jnp.float32
I32 = jnp.int32
VARS, NODES, LANES, HALO = 5, 64, 128, 32
SECTIONS, ROW, COLS = 4, 16, 8


def derivative_table():
    points = np.array([-1.0, -np.sqrt(0.2), np.sqrt(0.2), 1.0])
    weights = np.array([1.0 / np.prod([points[b] - points[c] for c in range(4) if c != b]) for b in range(4)])
    table = np.zeros((4, 4))
    for a in range(4):
        for b in range(4):
            if a != b:
                table[a, b] = weights[b] / weights[a] / (points[a] - points[b])
        table[a, a] = -np.sum(table[a])
    return table


def slope_matrix():
    table, eye = derivative_table().astype(np.float32).astype(np.float64), np.eye(4)
    parts = [np.eye(NODES)]
    for spots in ((table, eye, eye), (eye, table, eye), (eye, eye, table)):
        parts.append(np.kron(np.kron(spots[0], spots[1]), spots[2]))
    return np.concatenate(parts).astype(np.float32)


def dot(a, b):
    return jnp.dot(a, b, precision=lax.Precision.HIGHEST, preferred_element_type=F32)


def inverse_of(entries):
    left = [[entries[i][j] for j in range(4)] for i in range(4)]
    right = [[jnp.full_like(entries[0][0], 1.0 if i == j else 0.0) for j in range(4)] for i in range(4)]
    for pivot in range(4):
        scale = 1.0 / left[pivot][pivot]
        left[pivot] = [x * scale for x in left[pivot]]
        right[pivot] = [x * scale for x in right[pivot]]
        for target in range(4):
            if target != pivot:
                factor = left[target][pivot]
                left[target] = [x - factor * y for x, y in zip(left[target], left[pivot])]
                right[target] = [x - factor * y for x, y in zip(right[target], right[pivot])]
    return right


def pick(choices, which):
    out = choices[0]
    for i in range(1, len(choices)):
        out = jnp.where(which == i, choices[i], out)
    return out


def face_rows(u):
    sub = lax.broadcasted_iota(I32, (8, LANES), 0)
    low = sub < 4
    rows = [[u[0][0], u[0][1]], [u[3][0], u[3][1]], [], [], [], []]
    for h in range(2):
        a, b = u[2 * h], u[2 * h + 1]
        rows[2].append(jnp.where(low, a[0], pltpu.roll(b[0], 4, 0)))
        rows[3].append(jnp.where(low, pltpu.roll(a[1], 4, 0), b[1]))
    for f, k in ((4, 0), (5, 3)):
        at = k + 4 * (sub & 1)
        for h in range(2):
            a, b = u[2 * h], u[2 * h + 1]
            s = [jnp.take_along_axis(x, at, axis=0) for x in (a[0], a[1], b[0], b[1])]
            rows[f].append(jnp.where(low, jnp.where(sub < 2, s[0], s[1]), jnp.where(sub < 6, s[2], s[3])))
    return rows


def turned(a, b, code):
    swap = (code & 4) != 0
    a2 = jnp.where(swap, b, a)
    b2 = jnp.where(swap, a, b)
    a2 = jnp.where((code & 1) != 0, 3 - a2, a2)
    b2 = jnp.where((code & 2) != 0, 3 - b2, b2)
    return 4 * a2 + b2


def body(
    residual, transform, shifts, flux, penalty, block_inverse, nodal_inverse, neighbours, orientation, live_counts, slopes,
    out, rms,
    v_res, v_flux, v_pen, v_block, v_nodal, v_neigh, v_orient, v_slopes, s_transform, s_shift, s_live,
    n_all, mixed, blocks, pen_node, far_coef, far_row, own_at, halo_at, y, r, w, dirs, faces, near, pack, halo, red1, red2,
    in_sem, res_send, res_recv, pass_send, pass_recv, dir_send, dir_recv, across_send, across_recv, halo_send, halo_recv, red_send, red_recv, near_sem,
):
    s, e = lax.axis_index("section"), lax.axis_index("elem")
    x_peers = [(lax.rem(s + k, SECTIONS), e) for k in (1, 3, 2)]
    nxt, prv = (s, lax.rem(e + 1, 128)), (s, lax.rem(e + 127, 128))
    row_base = (e // ROW) * ROW
    row_at = e - row_base
    row_peers = [(s, row_base + lax.rem(row_at + k, ROW)) for k in (8, 9, 7, 6, 10, 5, 11, 4, 12, 3, 13, 2, 14, 15, 1)]
    plane_at = s * COLS + e // ROW
    plane_peers = []
    for k in (2, 1, 3, 0):
        for q in (4, 3, 5, 2, 6, 1, 7, 0):
            if k or q:
                plane_peers.append((lax.rem(s + k, SECTIONS), lax.rem(e + ROW * q, 128)))

    barrier = pltpu.get_barrier_semaphore()
    def along_row(k):
        return [(s, row_base + lax.rem(row_at + 2 * q, ROW)) for q in (k, COLS - k)]

    def along_column(k):
        return [(s, lax.rem(e + ROW * q, 128)) for q in (k, COLS - k)]

    peers = x_peers[:2] + [nxt, prv] + along_row(1) + along_column(1)
    for p in peers:
        pl.semaphore_signal(barrier, inc=1, device_id=p, device_id_type=MESH)
    rounds = [along_row(1), along_row(2), along_row(1), along_column(1), along_column(2), along_column(1)]

    def tell(n):
        for p in rounds[n]:
            pl.semaphore_signal(near_sem.at[n], inc=1, device_id=p, device_id_type=MESH)

    def hear(n):
        pl.semaphore_wait(near_sem.at[n], 2)


    loads = [
        (residual.at[0], v_res.at[s]), (flux, v_flux), (penalty, v_pen), (block_inverse, v_block), (nodal_inverse.at[0], v_nodal),
        (neighbours, v_neigh), (orientation, v_orient), (slopes, v_slopes), (transform, s_transform), (shifts, s_shift),
        (live_counts, s_live),
    ]
    loads = [pltpu.make_async_copy(a, b, in_sem.at[i]) for i, (a, b) in enumerate(loads)]
    for c in loads:
        c.start()

    pl.semaphore_wait(barrier, len(peers))
    sides = x_peers[:2]
    behind = [lax.rem(s + 3, SECTIONS), lax.rem(s + 1, SECTIONS)]
    res_copies = [[None] * VARS for _ in range(2)]
    for n in range(VARS):
        for d in range(2):
            k = n if d == 0 else VARS - 1 - n
            c = pltpu.make_async_remote_copy(
                src_ref=residual.at[0, k], dst_ref=v_res.at[s, k], send_sem=res_send.at[d, k], recv_sem=res_recv.at[d, k],
                device_id=sides[d], device_id_type=MESH,
            )
            c.start()
            res_copies[d][k] = c
    tell(0)
    for c in loads:
        c.wait()

    lane = lax.broadcasted_iota(I32, (8, LANES), 1)
    sub = lax.broadcasted_iota(I32, (8, LANES), 0)
    mask = jnp.where(lane < s_live[0], 1.0, 0.0).astype(F32)
    mask1 = mask[0:1]
    t_entries = [[jnp.full((8, LANES), s_transform[i, j], F32) for j in range(4)] for i in range(4)]
    inverse = inverse_of(t_entries)
    mix = [pick([inverse[i][t] for i in range(4)], s) * mask for t in range(4)]
    t_row = [pick([t_entries[i][t] for i in range(4)], s) for t in range(4)]

    n_full = dot(v_slopes[...], v_nodal[...])
    n_high = n_full.astype(jnp.bfloat16)
    n_all[0:4 * NODES, :] = n_high
    n_all[4 * NODES:8 * NODES, :] = (n_full - n_high.astype(F32)).astype(jnp.bfloat16)

    def spread(k, x):
        high = x.astype(jnp.bfloat16)
        low = (x - high.astype(F32)).astype(jnp.bfloat16)
        first = jnp.dot(n_all[...], high, preferred_element_type=F32)
        second = jnp.dot(n_all[0:4 * NODES, :], low, preferred_element_type=F32)
        y[k] = first[0:4 * NODES] + (first[4 * NODES:8 * NODES] + second)

    for m in range(VARS):
        blocks[m] = jnp.concatenate([v_block[m, c] for c in range(VARS)], axis=0) * mask1
    for d in range(3):
        for k in range(VARS):
            total = None
            for m in range(VARS):
                term = v_flux[k, m, d:d + 1, :] * blocks[m]
                total = term if total is None else total + term
            mixed[d, k] = total

    hear(0)
    tell(1)
    dead = jnp.zeros((8, LANES), F32)
    coef, code = [], []
    for f in range(6):
        far = jnp.broadcast_to(v_neigh[f:f + 1, :], (8, LANES))
        there = far >= 0
        at = far - e * LANES
        inside = there & (at >= 0) & (at < LANES)
        before = there & (at < 0)
        after = there & (at >= LANES)
        own_at[f] = jnp.where(inside, at, 0)
        halo_at[f] = jnp.where(before, at + HALO, jnp.where(after, at - LANES, 0))
        halo_at[6 + f] = jnp.where(before, 1, jnp.where(after, 2, 0))
        coef.append(jnp.where(there, jnp.broadcast_to(v_pen[f:f + 1, :], (8, LANES)), dead) * mask)
        code.append(jnp.broadcast_to(v_orient[f:f + 1, :], (8, LANES)))
    k_at, j_low = sub & 3, sub >> 2
    for n, (i, jh) in enumerate(((0, 0), (0, 1), (3, 0), (3, 1))):
        f = 0 if i == 0 else 1
        far_coef[n] = coef[f]
        far_row[n] = turned(2 * jh + j_low, k_at, code[f])
    for i in range(4):
        for jh in range(2):
            n = 4 + 2 * i + jh
            f = 2 + jh
            far_coef[n] = jnp.where(j_low == jh, coef[f], dead)
            far_row[n] = turned(jnp.full((8, LANES), i, I32), k_at, code[f])
            n += 8
            low_face = k_at < 2
            far_coef[n] = jnp.where(k_at == 0, coef[4], jnp.where(k_at == 3, coef[5], dead))
            far_row[n] = turned(jnp.full((8, LANES), i, I32), 2 * jh + j_low, jnp.where(low_face, code[4], code[5]))
    own_pen = [jnp.broadcast_to(v_pen[f:f + 1, :], (8, LANES)) for f in range(6)]
    for i in range(4):
        for jh in range(2):
            total = jnp.full((8, LANES), s_shift[0], F32)
            if i in (0, 3):
                total = total + own_pen[0 if i == 0 else 1]
            total = total + jnp.where(j_low == jh, own_pen[2 + jh], dead)
            total = total + jnp.where(k_at == 0, own_pen[4], jnp.where(k_at == 3, own_pen[5], dead))
            pen_node[2 * i + jh] = total

    hear(1)
    tell(2)
    passed = [[], []]
    for n in range(3):
        for d in range(2):
            k = n if d == 0 else VARS - 1 - n
            res_copies[d][k].wait_recv()
            rows = pl.ds(0, NODES) if n < 2 else pl.ds(NODES // 2 * d, NODES // 2)
            part = v_res.at[behind[d], k, rows]
            c = pltpu.make_async_remote_copy(
                src_ref=part, dst_ref=part, send_sem=pass_send.at[d, n], recv_sem=pass_recv.at[d, n], device_id=sides[d],
                device_id_type=MESH,
            )
            c.start()
            passed[d].append(c)
    hear(2)
    tell(3)
    for k in (0, 4, 1, 3, 2):
        if k < 2:
            res_copies[1][k].wait_recv()
            passed[0][k].wait_recv()
        elif k > 2:
            res_copies[0][k].wait_recv()
            passed[1][VARS - 1 - k].wait_recv()
        else:
            passed[0][2].wait_recv()
            passed[1][2].wait_recv()
        for q in range(8):
            rows = pl.ds(8 * q, 8)
            total = mix[0] * v_res[0, k, rows, :]
            for t in range(1, 4):
                total = total + mix[t] * v_res[t, k, rows, :]
            r[k, rows, :] = total
        spread(k, r[k])

    dir_copies, across_copies, halo_copies = [], [], []

    def pass_on(step):
        for d in range(2):
            dir_copies[2 * step + d].wait_recv()
            part = dirs.at[step, behind[d], pl.ds(0, VARS), pl.ds(NODES // 2 * d, NODES // 2)]
            c = pltpu.make_async_remote_copy(
                src_ref=part, dst_ref=part, send_sem=across_send.at[step, d], recv_sem=across_recv.at[step, d],
                device_id=sides[d], device_id_type=MESH,
            )
            c.start()
            across_copies.append(c)

    def operator(step, target):
        for k in range(VARS):
            total = None
            for c in range(VARS):
                term = blocks[k, c:c + 1, :] * y[c, 0:NODES, :]
                total = term if total is None else total + term
            dirs[step, s, k] = total
        for k in range(VARS):
            u = [[dirs[step, s, k, pl.ds(16 * i + 8 * jh, 8), :] for jh in range(2)] for i in range(4)]
            rows = face_rows(u)
            for f in range(6):
                for h in range(2):
                    faces[f * 10 + k * 2 + h] = rows[f][h]
        group = lane >> 5
        for p in range(15):
            x = [faces[4 * p + g] for g in range(4)]
            x = [x[0]] + [pltpu.roll(x[g], 32 * g, 1) for g in range(1, 4)]
            pack[step, 0, p] = jnp.where(group < 2, jnp.where(group == 0, x[0], x[1]), jnp.where(group == 2, x[2], x[3]))
            pack[step, 1, p] = jnp.where(group < 2, jnp.where(group == 0, x[1], x[2]), jnp.where(group == 2, x[3], x[0]))
        waits = []
        for side, p in ((0, prv), (1, nxt)):
            c = pltpu.make_async_remote_copy(
                src_ref=pack.at[step, side], dst_ref=halo.at[step, side], send_sem=halo_send.at[step, side],
                recv_sem=halo_recv.at[step, side], device_id=p, device_id_type=MESH,
            )
            c.start()
            waits.append(c)
            halo_copies.append(c)
        for d in range(2):
            c = pltpu.make_async_remote_copy(
                src_ref=dirs.at[step, s], dst_ref=dirs.at[step, s], send_sem=dir_send.at[step, d],
                recv_sem=dir_recv.at[step, d], device_id=sides[d], device_id_type=MESH,
            )
            c.start()
            dir_copies.append(c)
        if step == 1:
            pass_on(0)
        for k in range(VARS):
            total = jnp.concatenate([pen_node[q] for q in range(8)], axis=0) * dirs[step, s, k]
            for d in range(3):
                for c in range(VARS):
                    total = total + mixed[d, k, c:c + 1, :] * y[c, NODES * (d + 1):NODES * (d + 2), :]
            target[k] = total
        for f in range(6):
            at = own_at[f]
            for n in range(10):
                near[f * 10 + n] = jnp.take_along_axis(faces[(f ^ 1) * 10 + n], at, axis=1)
        hear(3 + step)
        tell(4 + step)
        for c in waits:
            c.wait_recv()
        for f in range(6):
            at = halo_at[f]
            side = halo_at[6 + f]
            for n in range(10):
                m = (f ^ 1) * 10 + n
                p, g = m // 4, m % 4
                after = jnp.take_along_axis(halo[step, 0, p], at + 32 * g, axis=1)
                before = jnp.take_along_axis(halo[step, 1, p], at + 32 * ((g + 3) % 4), axis=1)
                near[f * 10 + n] = jnp.where(side == 0, near[f * 10 + n], jnp.where(side == 1, before, after))
        for n in range(20):
            row = far_row[n]
            at, high = row & 7, row >= 8
            if n < 4:
                f, i, jh = n // 2, 3 * (n // 2), n % 2
            else:
                i, jh = ((n - 4) % 8) // 2, n % 2
                f = 2 + jh if n < 12 else 4
            for k in range(VARS):
                def turn(face):
                    a = jnp.take_along_axis(near[face * 10 + 2 * k], at, axis=0)
                    b = jnp.take_along_axis(near[face * 10 + 2 * k + 1], at, axis=0)
                    return jnp.where(high, b, a)

                far = turn(f) if f < 4 else jnp.where(k_at < 2, turn(4), turn(5))
                rows = pl.ds(16 * i + 8 * jh, 8)
                target[k, rows, :] = target[k, rows, :] - far_coef[n] * far

    operator(0, w.at[0])
    for k in range(VARS):
        spread(k, w[0, k])
    operator(1, w.at[1])

    sums = [None] * 6
    for k in range(VARS):
        for q in range(8):
            rows = pl.ds(8 * q, 8)
            a, b, c = r[k, rows, :], w[0, k, rows, :], w[1, k, rows, :]
            for n, term in enumerate((a * a, a * b, b * b, a * c, b * c, c * c)):
                sums[n] = term if sums[n] is None else sums[n] + term
    stacked = dead
    for n in range(6):
        stacked = jnp.where(sub == n, jnp.sum(sums[n], axis=0, keepdims=True), stacked)
    stacked = jnp.where(sub == lane, jnp.sum(stacked, axis=1, keepdims=True), dead)
    hear(5)
    red1[row_at] = jnp.sum(stacked, axis=0, keepdims=True)
    for p in row_peers:
        pltpu.make_async_remote_copy(
            src_ref=red1.at[row_at], dst_ref=red1.at[row_at], send_sem=red_send.at[0], recv_sem=red_recv.at[0], device_id=p,
            device_id_type=MESH,
        ).start()
    all_row = pltpu.make_async_remote_copy(
        src_ref=red1.at[pl.ds(0, ROW - 1)], dst_ref=red1.at[pl.ds(0, ROW - 1)], send_sem=red_send.at[0],
        recv_sem=red_recv.at[0], device_id=prv, device_id_type=MESH,
    )
    pass_on(1)
    all_row.wait_recv()
    total = red1[0]
    for n in range(1, ROW):
        total = total + red1[n]
    red2[plane_at] = total
    for p in plane_peers:
        pltpu.make_async_remote_copy(
            src_ref=red2.at[plane_at], dst_ref=red2.at[plane_at], send_sem=red_send.at[1], recv_sem=red_recv.at[1],
            device_id=p, device_id_type=MESH,
        ).start()
    count = SECTIONS * COLS - 1
    all_plane = pltpu.make_async_remote_copy(
        src_ref=red2.at[pl.ds(0, count)], dst_ref=red2.at[pl.ds(0, count)], send_sem=red_send.at[1],
        recv_sem=red_recv.at[1], device_id=prv, device_id_type=MESH,
    )
    all_plane.wait_recv()
    one, two = [], []
    start = None
    for t in range(SECTIONS):
        total = red2[COLS * t]
        for n in range(1, COLS):
            total = total + red2[COLS * t + n]
        g = [jnp.sum(jnp.where(lane[0:1] == n, total, 0.0), axis=1, keepdims=True) for n in range(6)]
        ratio = g[4] / g[2]
        c2 = (g[3] - ratio * g[1]) / (g[5] - ratio * g[4])
        c1 = g[1] / g[2] - ratio * c2
        one.append(t_row[t] * c1)
        two.append(t_row[t] * c2)
        start = g[0] if start is None else jnp.where(s == t, g[0], start)
    rms[...] = jnp.broadcast_to(jnp.sqrt(start) / np.float32(np.sqrt(np.float32(VARS * NODES * LANES * 128))), rms.shape)
    for c in across_copies:
        c.wait_recv()
    for k in range(VARS):
        for q in range(8):
            rows = pl.ds(8 * q, 8)
            total = None
            for t in range(SECTIONS):
                term = one[t] * dirs[0, t, k, rows, :] + two[t] * dirs[1, t, k, rows, :]
                total = term if total is None else total + term
            out[0, k, rows, :] = total
    for c in res_copies[0] + res_copies[1] + passed[0] + passed[1] + dir_copies + across_copies + halo_copies + [all_row, all_plane]:
        c.wait_send()


def local(*args):
    hbm = pl.BlockSpec(memory_space=pltpu.HBM)
    ANY = pl.BlockSpec(memory_space=pl.ANY)
    vmem = pl.BlockSpec(memory_space=pltpu.VMEM)
    dma = pltpu.SemaphoreType.DMA
    slopes = jnp.asarray(slope_matrix())
    args = list(args)
    args[3] = jnp.transpose(args[3], (1, 2, 0, 3))
    args[5] = jnp.transpose(args[5], (1, 2, 0, 3))
    update, rms = pl.pallas_call(
        body,
        out_shape=(
            pltpu.VMEM((1, VARS, NODES, LANES), F32),
            pltpu.VMEM((1, LANES), F32),
        ),
        in_specs=[hbm, hbm, ANY] + [hbm] * 6 + [ANY, hbm],
        out_specs=(vmem, vmem),
        scratch_shapes=[
            pltpu.VMEM((SECTIONS, VARS, NODES, LANES), F32),
            pltpu.VMEM((VARS, VARS, 3, LANES), F32),
            pltpu.VMEM((6, LANES), F32),
            pltpu.VMEM((VARS, VARS, 1, LANES), F32),
            pltpu.VMEM((NODES, NODES), F32),
            pltpu.VMEM((6, LANES), I32),
            pltpu.VMEM((6, LANES), I32),
            pltpu.VMEM((4 * NODES, NODES), F32),
            pltpu.SMEM((4, 4), F32),
            pltpu.SMEM((1,), F32),
            pltpu.SMEM((1,), I32),
            pltpu.VMEM((8 * NODES, NODES), jnp.bfloat16),
            pltpu.VMEM((3, VARS, VARS, LANES), F32),
            pltpu.VMEM((VARS, VARS, LANES), F32),
            pltpu.VMEM((8, 8, LANES), F32),
            pltpu.VMEM((20, 8, LANES), F32),
            pltpu.VMEM((20, 8, LANES), I32),
            pltpu.VMEM((6, 8, LANES), I32),
            pltpu.VMEM((12, 8, LANES), I32),
            pltpu.VMEM((VARS, 4 * NODES, LANES), F32),
            pltpu.VMEM((VARS, NODES, LANES), F32),
            pltpu.VMEM((2, VARS, NODES, LANES), F32),
            pltpu.VMEM((2, SECTIONS, VARS, NODES, LANES), F32),
            pltpu.VMEM((60, 8, LANES), F32),
            pltpu.VMEM((60, 8, LANES), F32),
            pltpu.VMEM((2, 2, 15, 8, LANES), F32),
            pltpu.VMEM((2, 2, 15, 8, LANES), F32),
            pltpu.VMEM((ROW, 1, LANES), F32),
            pltpu.VMEM((SECTIONS * COLS, 1, LANES), F32),
            dma((11,)), dma((2, VARS)), dma((2, VARS)), dma((2, 3)), dma((2, 3)), dma((2, 2)), dma((2, 2)), dma((2, 2)), dma((2, 2)),
            dma((2, 2)), dma((2, 2)), dma((2,)), dma((2,)), pltpu.SemaphoreType.REGULAR((6,)),
        ],
        compiler_params=pltpu.CompilerParams(collective_id=0, has_side_effects=True, vmem_limit_bytes=32 * 1024 * 1024),
        name="newton_step",
    )(*[x if x.shape == (1,) else pltpu.with_memory_space_constraint(x, pltpu.HBM) for x in args + [slopes]])
    return update, rms[0, 0:1]


def solution(mesh):
    placed = (
        P("section", None, None, "elem"), P(), P("section"), P(None, None, None, "elem"), P(None, "elem"),
        P("section", None, None, "elem"), P("section", None, None), P(None, "elem"), P(None, "elem"), P("elem"),
    )
    return jax.shard_map(
        local, mesh=mesh, in_specs=placed, out_specs=(P("section", None, None, "elem"), P("section")), check_vma=False,
    )
```

```python
import functools

import jax
import jax.numpy as jnp
import numpy as np
from jax import lax
from jax.experimental import pallas as pl
from jax.experimental.pallas import tpu as pltpu
from jax.sharding import PartitionSpec as P

MESH = pl.DeviceIdType.MESH
F32 = jnp.float32
I32 = jnp.int32
VARS, NODES, LANES, HALO = 5, 64, 128, 32
SECTIONS, ROW, COLS = 4, 16, 8


def derivative_table():
    points = np.array([-1.0, -np.sqrt(0.2), np.sqrt(0.2), 1.0])
    weights = np.array([1.0 / np.prod([points[b] - points[c] for c in range(4) if c != b]) for b in range(4)])
    table = np.zeros((4, 4))
    for a in range(4):
        for b in range(4):
            if a != b:
                table[a, b] = weights[b] / weights[a] / (points[a] - points[b])
        table[a, a] = -np.sum(table[a])
    return table


def slope_matrix():
    table, eye = derivative_table().astype(np.float32).astype(np.float64), np.eye(4)
    parts = [np.eye(NODES)]
    for spots in ((table, eye, eye), (eye, table, eye), (eye, eye, table)):
        parts.append(np.kron(np.kron(spots[0], spots[1]), spots[2]))
    return np.concatenate(parts).astype(np.float32)


def dot(a, b):
    return jnp.dot(a, b, precision=lax.Precision.HIGHEST, preferred_element_type=F32)


def inverse_of(entries):
    left = [[entries[i][j] for j in range(4)] for i in range(4)]
    right = [[jnp.full_like(entries[0][0], 1.0 if i == j else 0.0) for j in range(4)] for i in range(4)]
    for pivot in range(4):
        scale = 1.0 / left[pivot][pivot]
        left[pivot] = [x * scale for x in left[pivot]]
        right[pivot] = [x * scale for x in right[pivot]]
        for target in range(4):
            if target != pivot:
                factor = left[target][pivot]
                left[target] = [x - factor * y for x, y in zip(left[target], left[pivot])]
                right[target] = [x - factor * y for x, y in zip(right[target], right[pivot])]
    return right


def pick(choices, which):
    out = choices[0]
    for i in range(1, len(choices)):
        out = jnp.where(which == i, choices[i], out)
    return out


def face_rows(u):
    sub = lax.broadcasted_iota(I32, (8, LANES), 0)
    low = sub < 4
    rows = [[u[0][0], u[0][1]], [u[3][0], u[3][1]], [], [], [], []]
    for h in range(2):
        a, b = u[2 * h], u[2 * h + 1]
        rows[2].append(jnp.where(low, a[0], pltpu.roll(b[0], 4, 0)))
        rows[3].append(jnp.where(low, pltpu.roll(a[1], 4, 0), b[1]))
    for f, k in ((4, 0), (5, 3)):
        at = k + 4 * (sub & 1)
        for h in range(2):
            a, b = u[2 * h], u[2 * h + 1]
            s = [jnp.take_along_axis(x, at, axis=0) for x in (a[0], a[1], b[0], b[1])]
            rows[f].append(jnp.where(low, jnp.where(sub < 2, s[0], s[1]), jnp.where(sub < 6, s[2], s[3])))
    return rows


def turned(a, b, code):
    swap = (code & 4) != 0
    a2 = jnp.where(swap, b, a)
    b2 = jnp.where(swap, a, b)
    a2 = jnp.where((code & 1) != 0, 3 - a2, a2)
    b2 = jnp.where((code & 2) != 0, 3 - b2, b2)
    return 4 * a2 + b2


def body(
    residual, transform, shifts, flux, penalty, block_inverse, nodal_inverse, neighbours, orientation, live_counts, slopes,
    out, rms,
    v_res, v_flux, v_pen, v_block, v_nodal, v_neigh, v_orient, v_slopes, s_transform, s_shift, s_live,
    n_all, mixed, blocks, pen_node, far_coef, far_row, own_at, halo_at, y, r, w, dirs, faces, near, pack, halo, red1, red2,
    in_sem, res_send, res_recv, pass_send, pass_recv, dir_send, dir_recv, across_send, across_recv, halo_send, halo_recv, red_send, red_recv, near_sem,
):
    s, e = lax.axis_index("section"), lax.axis_index("elem")
    x_peers = [(lax.rem(s + k, SECTIONS), e) for k in (1, 3, 2)]
    nxt, prv = (s, lax.rem(e + 1, 128)), (s, lax.rem(e + 127, 128))
    row_base = (e // ROW) * ROW
    row_at = e - row_base
    row_peers = [(s, row_base + lax.rem(row_at + k, ROW)) for k in (8, 9, 7, 6, 10, 5, 11, 4, 12, 3, 13, 2, 14, 15, 1)]
    plane_at = s * COLS + e // ROW
    plane_peers = []
    for k in (2, 1, 3, 0):
        for q in (4, 3, 5, 2, 6, 1, 7, 0):
            if k or q:
                plane_peers.append((lax.rem(s + k, SECTIONS), lax.rem(e + ROW * q, 128)))

    barrier = pltpu.get_barrier_semaphore()
    def along_row(k):
        return [(s, row_base + lax.rem(row_at + 2 * q, ROW)) for q in (k, COLS - k)]

    def along_column(k):
        return [(s, lax.rem(e + ROW * q, 128)) for q in (k, COLS - k)]

    peers = x_peers[:2] + [nxt, prv] + along_row(1) + along_column(1)
    for p in peers:
        pl.semaphore_signal(barrier, inc=1, device_id=p, device_id_type=MESH)
    rounds = [along_row(1), along_row(2), along_row(1), along_column(1), along_column(2), along_column(1)]

    def tell(n):
        for p in rounds[n]:
            pl.semaphore_signal(near_sem.at[n], inc=1, device_id=p, device_id_type=MESH)

    def hear(n):
        pl.semaphore_wait(near_sem.at[n], 2)


    loads = [
        (residual.at[0], v_res.at[s]), (flux, v_flux), (penalty, v_pen), (block_inverse, v_block), (nodal_inverse.at[0], v_nodal),
        (neighbours, v_neigh), (orientation, v_orient), (slopes, v_slopes), (transform, s_transform), (shifts, s_shift),
        (live_counts, s_live),
    ]
    loads = [pltpu.make_async_copy(a, b, in_sem.at[i]) for i, (a, b) in enumerate(loads)]
    for c in loads:
        c.start()

    pl.semaphore_wait(barrier, len(peers))
    sides = x_peers[:2]
    behind = [lax.rem(s + 3, SECTIONS), lax.rem(s + 1, SECTIONS)]
    res_copies = [[None] * VARS for _ in range(2)]
    for n in range(VARS):
        for d in range(2):
            k = n if d == 0 else VARS - 1 - n
            c = pltpu.make_async_remote_copy(
                src_ref=residual.at[0, k], dst_ref=v_res.at[s, k], send_sem=res_send.at[d, k], recv_sem=res_recv.at[d, k],
                device_id=sides[d], device_id_type=MESH,
            )
            c.start()
            res_copies[d][k] = c
    tell(0)
    for c in loads:
        c.wait()

    lane = lax.broadcasted_iota(I32, (8, LANES), 1)
    sub = lax.broadcasted_iota(I32, (8, LANES), 0)
    mask = jnp.where(lane < s_live[0], 1.0, 0.0).astype(F32)
    mask1 = mask[0:1]
    t_entries = [[jnp.full((8, LANES), s_transform[i, j], F32) for j in range(4)] for i in range(4)]
    inverse = inverse_of(t_entries)
    size = [jnp.maximum(sum(jnp.abs(x) for x in row), 1.0) for row in inverse]
    own_size = pick(size, s)
    scale = mask / own_size
    mix = [pick([inverse[i][t] for i in range(4)], s) * scale for t in range(4)]
    t_row = [pick([t_entries[i][t] for i in range(4)], s) * size[t] for t in range(4)]

    n_full = dot(v_slopes[...], v_nodal[...])
    n_high = n_full.astype(jnp.bfloat16)
    n_all[0:4 * NODES, :] = n_high
    n_all[4 * NODES:8 * NODES, :] = (n_full - n_high.astype(F32)).astype(jnp.bfloat16)

    def spread(k, x):
        high = x.astype(jnp.bfloat16)
        low = (x - high.astype(F32)).astype(jnp.bfloat16)
        first = jnp.dot(n_all[...], high, preferred_element_type=F32)
        second = jnp.dot(n_all[0:4 * NODES, :], low, preferred_element_type=F32)
        y[k] = first[0:4 * NODES] + (first[4 * NODES:8 * NODES] + second)

    for m in range(VARS):
        blocks[m] = jnp.concatenate([v_block[m, c] for c in range(VARS)], axis=0) * mask1
    for d in range(3):
        for k in range(VARS):
            total = None
            for m in range(VARS):
                term = v_flux[k, m, d:d + 1, :] * blocks[m]
                total = term if total is None else total + term
            mixed[d, k] = total

    hear(0)
    tell(1)
    passed = [[], []]
    for n in range(3):
        for d in range(2):
            k = n if d == 0 else VARS - 1 - n
            res_copies[d][k].wait_recv()
            rows = pl.ds(0, NODES) if n < 2 else pl.ds(NODES // 2 * d, NODES // 2)
            part = v_res.at[behind[d], k, rows]
            c = pltpu.make_async_remote_copy(
                src_ref=part, dst_ref=part, send_sem=pass_send.at[d, n], recv_sem=pass_recv.at[d, n], device_id=sides[d],
                device_id_type=MESH,
            )
            c.start()
            passed[d].append(c)
    hear(1)
    tell(2)
    dead = jnp.zeros((8, LANES), F32)
    coef, code = [], []
    for f in range(6):
        far = jnp.broadcast_to(v_neigh[f:f + 1, :], (8, LANES))
        there = far >= 0
        at = far - e * LANES
        inside = there & (at >= 0) & (at < LANES)
        before = there & (at < 0)
        after = there & (at >= LANES)
        own_at[f] = jnp.where(inside, at, 0)
        halo_at[f] = jnp.where(before, at + HALO, jnp.where(after, at - LANES, 0))
        halo_at[6 + f] = jnp.where(before, 1, jnp.where(after, 2, 0))
        coef.append(jnp.where(there, jnp.broadcast_to(v_pen[f:f + 1, :], (8, LANES)), dead) * mask)
        code.append(jnp.broadcast_to(v_orient[f:f + 1, :], (8, LANES)))
    k_at, j_low = sub & 3, sub >> 2
    for n, (i, jh) in enumerate(((0, 0), (0, 1), (3, 0), (3, 1))):
        f = 0 if i == 0 else 1
        far_coef[n] = coef[f]
        far_row[n] = turned(2 * jh + j_low, k_at, code[f])
    for i in range(4):
        for jh in range(2):
            n = 4 + 2 * i + jh
            f = 2 + jh
            far_coef[n] = jnp.where(j_low == jh, coef[f], dead)
            far_row[n] = turned(jnp.full((8, LANES), i, I32), k_at, code[f])
            n += 8
            low_face = k_at < 2
            far_coef[n] = jnp.where(k_at == 0, coef[4], jnp.where(k_at == 3, coef[5], dead))
            far_row[n] = turned(jnp.full((8, LANES), i, I32), 2 * jh + j_low, jnp.where(low_face, code[4], code[5]))
    own_pen = [jnp.broadcast_to(v_pen[f:f + 1, :], (8, LANES)) for f in range(6)]
    for i in range(4):
        for jh in range(2):
            total = jnp.full((8, LANES), s_shift[0], F32)
            if i in (0, 3):
                total = total + own_pen[0 if i == 0 else 1]
            total = total + jnp.where(j_low == jh, own_pen[2 + jh], dead)
            total = total + jnp.where(k_at == 0, own_pen[4], jnp.where(k_at == 3, own_pen[5], dead))
            pen_node[2 * i + jh] = total

    hear(2)
    tell(3)
    for k in (0, 4, 1, 3, 2):
        if k < 2:
            res_copies[1][k].wait_recv()
            passed[0][k].wait_recv()
        elif k > 2:
            res_copies[0][k].wait_recv()
            passed[1][VARS - 1 - k].wait_recv()
        else:
            passed[0][2].wait_recv()
            passed[1][2].wait_recv()
        for q in range(8):
            rows = pl.ds(8 * q, 8)
            total = mix[0] * v_res[0, k, rows, :]
            for t in range(1, 4):
                total = total + mix[t] * v_res[t, k, rows, :]
            r[k, rows, :] = total
        spread(k, r[k])

    dir_copies, across_copies, halo_copies = [], [], []

    def pass_on(step):
        for d in range(2):
            dir_copies[2 * step + d].wait_recv()
            part = dirs.at[step, behind[d], pl.ds(0, VARS), pl.ds(NODES // 2 * d, NODES // 2)]
            c = pltpu.make_async_remote_copy(
                src_ref=part, dst_ref=part, send_sem=across_send.at[step, d], recv_sem=across_recv.at[step, d],
                device_id=sides[d], device_id_type=MESH,
            )
            c.start()
            across_copies.append(c)

    def operator(step, target):
        for k in range(VARS):
            total = None
            for c in range(VARS):
                term = blocks[k, c:c + 1, :] * y[c, 0:NODES, :]
                total = term if total is None else total + term
            dirs[step, s, k] = total
        for k in range(VARS):
            u = [[dirs[step, s, k, pl.ds(16 * i + 8 * jh, 8), :] for jh in range(2)] for i in range(4)]
            rows = face_rows(u)
            for f in range(6):
                for h in range(2):
                    faces[f * 10 + k * 2 + h] = rows[f][h]
        group = lane >> 5
        for p in range(15):
            x = [faces[4 * p + g] for g in range(4)]
            x = [x[0]] + [pltpu.roll(x[g], 32 * g, 1) for g in range(1, 4)]
            pack[step, 0, p] = jnp.where(group < 2, jnp.where(group == 0, x[0], x[1]), jnp.where(group == 2, x[2], x[3]))
            pack[step, 1, p] = jnp.where(group < 2, jnp.where(group == 0, x[1], x[2]), jnp.where(group == 2, x[3], x[0]))
        waits = []
        for side, p in ((0, prv), (1, nxt)):
            c = pltpu.make_async_remote_copy(
                src_ref=pack.at[step, side], dst_ref=halo.at[step, side], send_sem=halo_send.at[step, side],
                recv_sem=halo_recv.at[step, side], device_id=p, device_id_type=MESH,
            )
            c.start()
            waits.append(c)
            halo_copies.append(c)
        for d in range(2):
            c = pltpu.make_async_remote_copy(
                src_ref=dirs.at[step, s], dst_ref=dirs.at[step, s], send_sem=dir_send.at[step, d],
                recv_sem=dir_recv.at[step, d], device_id=sides[d], device_id_type=MESH,
            )
            c.start()
            dir_copies.append(c)
        if step == 1:
            pass_on(0)
        for k in range(VARS):
            total = jnp.concatenate([pen_node[q] for q in range(8)], axis=0) * dirs[step, s, k]
            for d in range(3):
                for c in range(VARS):
                    total = total + mixed[d, k, c:c + 1, :] * y[c, NODES * (d + 1):NODES * (d + 2), :]
            target[k] = total
        for f in range(6):
            at = own_at[f]
            for n in range(10):
                near[f * 10 + n] = jnp.take_along_axis(faces[(f ^ 1) * 10 + n], at, axis=1)
        hear(3 + step)
        tell(4 + step)
        for c in waits:
            c.wait_recv()
        for f in range(6):
            at = halo_at[f]
            side = halo_at[6 + f]
            for n in range(10):
                m = (f ^ 1) * 10 + n
                p, g = m // 4, m % 4
                after = jnp.take_along_axis(halo[step, 0, p], at + 32 * g, axis=1)
                before = jnp.take_along_axis(halo[step, 1, p], at + 32 * ((g + 3) % 4), axis=1)
                near[f * 10 + n] = jnp.where(side == 0, near[f * 10 + n], jnp.where(side == 1, before, after))
        for n in range(20):
            row = far_row[n]
            at, high = row & 7, row >= 8
            if n < 4:
                f, i, jh = n // 2, 3 * (n // 2), n % 2
            else:
                i, jh = ((n - 4) % 8) // 2, n % 2
                f = 2 + jh if n < 12 else 4
            for k in range(VARS):
                def turn(face):
                    a = jnp.take_along_axis(near[face * 10 + 2 * k], at, axis=0)
                    b = jnp.take_along_axis(near[face * 10 + 2 * k + 1], at, axis=0)
                    return jnp.where(high, b, a)

                far = turn(f) if f < 4 else jnp.where(k_at < 2, turn(4), turn(5))
                rows = pl.ds(16 * i + 8 * jh, 8)
                target[k, rows, :] = target[k, rows, :] - far_coef[n] * far

    operator(0, w.at[0])
    for k in range(VARS):
        spread(k, w[0, k])
    operator(1, w.at[1])

    sums = [None] * 6
    for k in range(VARS):
        for q in range(8):
            rows = pl.ds(8 * q, 8)
            a, b, c = r[k, rows, :], w[0, k, rows, :], w[1, k, rows, :]
            for n, term in enumerate((a * a, a * b, b * b, a * c, b * c, c * c)):
                sums[n] = term if sums[n] is None else sums[n] + term
    stacked = dead
    for n in range(6):
        stacked = jnp.where(sub == n, jnp.sum(sums[n], axis=0, keepdims=True), stacked)
    stacked = jnp.where(sub == lane, jnp.sum(stacked, axis=1, keepdims=True), dead)
    hear(5)
    red1[row_at] = jnp.sum(stacked, axis=0, keepdims=True)
    for p in row_peers:
        pltpu.make_async_remote_copy(
            src_ref=red1.at[row_at], dst_ref=red1.at[row_at], send_sem=red_send.at[0], recv_sem=red_recv.at[0], device_id=p,
            device_id_type=MESH,
        ).start()
    all_row = pltpu.make_async_remote_copy(
        src_ref=red1.at[pl.ds(0, ROW - 1)], dst_ref=red1.at[pl.ds(0, ROW - 1)], send_sem=red_send.at[0],
        recv_sem=red_recv.at[0], device_id=prv, device_id_type=MESH,
    )
    pass_on(1)
    all_row.wait_recv()
    total = red1[0]
    for n in range(1, ROW):
        total = total + red1[n]
    red2[plane_at] = total
    for p in plane_peers:
        pltpu.make_async_remote_copy(
            src_ref=red2.at[plane_at], dst_ref=red2.at[plane_at], send_sem=red_send.at[1], recv_sem=red_recv.at[1],
            device_id=p, device_id_type=MESH,
        ).start()
    count = SECTIONS * COLS - 1
    all_plane = pltpu.make_async_remote_copy(
        src_ref=red2.at[pl.ds(0, count)], dst_ref=red2.at[pl.ds(0, count)], send_sem=red_send.at[1],
        recv_sem=red_recv.at[1], device_id=prv, device_id_type=MESH,
    )
    all_plane.wait_recv()
    totals = []
    for t in range(SECTIONS):
        total = red2[COLS * t]
        for n in range(1, COLS):
            total = total + red2[COLS * t + n]
        totals.append(total)
    totals = jnp.concatenate(totals, axis=0)
    g = [jnp.sum(jnp.where(lane[0:SECTIONS] == n, totals, 0.0), axis=1, keepdims=True) for n in range(6)]
    ratio = g[4] / g[2]
    c2 = (g[3] - ratio * g[1]) / (g[5] - ratio * g[4])
    c1 = g[1] / g[2] - ratio * c2
    one = [t_row[t] * c1[t:t + 1] for t in range(SECTIONS)]
    two = [t_row[t] * c2[t:t + 1] for t in range(SECTIONS)]
    start = jnp.sum(jnp.where(lax.broadcasted_iota(I32, (SECTIONS, 1), 0) == s, g[0], 0.0), axis=0, keepdims=True)
    rms[...] = own_size[0:1] * (jnp.sqrt(start) / np.float32(np.sqrt(np.float32(VARS * NODES * LANES * 128))))
    for c in across_copies:
        c.wait_recv()
    for k in range(VARS):
        for q in range(8):
            rows = pl.ds(8 * q, 8)
            total = None
            for t in range(SECTIONS):
                term = one[t] * dirs[0, t, k, rows, :] + two[t] * dirs[1, t, k, rows, :]
                total = term if total is None else total + term
            out[0, k, rows, :] = total
    for c in res_copies[0] + res_copies[1] + passed[0] + passed[1] + dir_copies + across_copies + halo_copies + [all_row, all_plane]:
        c.wait_send()


def local(*args):
    hbm = pl.BlockSpec(memory_space=pltpu.HBM)
    ANY = pl.BlockSpec(memory_space=pl.ANY)
    vmem = pl.BlockSpec(memory_space=pltpu.VMEM)
    dma = pltpu.SemaphoreType.DMA
    slopes = jnp.asarray(slope_matrix())
    args = list(args)
    args[3] = jnp.transpose(args[3], (1, 2, 0, 3))
    args[5] = jnp.transpose(args[5], (1, 2, 0, 3))
    update, rms = pl.pallas_call(
        body,
        out_shape=(
            pltpu.VMEM((1, VARS, NODES, LANES), F32),
            pltpu.VMEM((1, LANES), F32),
        ),
        in_specs=[hbm, hbm, ANY] + [hbm] * 6 + [ANY, hbm],
        out_specs=(vmem, vmem),
        scratch_shapes=[
            pltpu.VMEM((SECTIONS, VARS, NODES, LANES), F32),
            pltpu.VMEM((VARS, VARS, 3, LANES), F32),
            pltpu.VMEM((6, LANES), F32),
            pltpu.VMEM((VARS, VARS, 1, LANES), F32),
            pltpu.VMEM((NODES, NODES), F32),
            pltpu.VMEM((6, LANES), I32),
            pltpu.VMEM((6, LANES), I32),
            pltpu.VMEM((4 * NODES, NODES), F32),
            pltpu.SMEM((4, 4), F32),
            pltpu.SMEM((1,), F32),
            pltpu.SMEM((1,), I32),
            pltpu.VMEM((8 * NODES, NODES), jnp.bfloat16),
            pltpu.VMEM((3, VARS, VARS, LANES), F32),
            pltpu.VMEM((VARS, VARS, LANES), F32),
            pltpu.VMEM((8, 8, LANES), F32),
            pltpu.VMEM((20, 8, LANES), F32),
            pltpu.VMEM((20, 8, LANES), I32),
            pltpu.VMEM((6, 8, LANES), I32),
            pltpu.VMEM((12, 8, LANES), I32),
            pltpu.VMEM((VARS, 4 * NODES, LANES), F32),
            pltpu.VMEM((VARS, NODES, LANES), F32),
            pltpu.VMEM((2, VARS, NODES, LANES), F32),
            pltpu.VMEM((2, SECTIONS, VARS, NODES, LANES), F32),
            pltpu.VMEM((60, 8, LANES), F32),
            pltpu.VMEM((60, 8, LANES), F32),
            pltpu.VMEM((2, 2, 15, 8, LANES), F32),
            pltpu.VMEM((2, 2, 15, 8, LANES), F32),
            pltpu.VMEM((ROW, 1, LANES), F32),
            pltpu.VMEM((SECTIONS * COLS, 1, LANES), F32),
            dma((11,)), dma((2, VARS)), dma((2, VARS)), dma((2, 3)), dma((2, 3)), dma((2, 2)), dma((2, 2)), dma((2, 2)), dma((2, 2)),
            dma((2, 2)), dma((2, 2)), dma((2,)), dma((2,)), pltpu.SemaphoreType.REGULAR((6,)),
        ],
        compiler_params=pltpu.CompilerParams(collective_id=0, has_side_effects=True, vmem_limit_bytes=32 * 1024 * 1024),
        name="newton_step",
    )(*[x if x.shape == (1,) else pltpu.with_memory_space_constraint(x, pltpu.HBM) for x in args + [slopes]])
    return update, rms[0, 0:1]


def solution(mesh):
    placed = (
        P("section", None, None, "elem"), P(), P("section"), P(None, None, None, "elem"), P(None, "elem"),
        P("section", None, None, "elem"), P("section", None, None), P(None, "elem"), P(None, "elem"), P("elem"),
    )
    return jax.shard_map(
        local, mesh=mesh, in_specs=placed, out_specs=(P("section", None, None, "elem"), P("section")), check_vma=False,
    )
```

```python
import functools

import jax
import jax.numpy as jnp
import numpy as np
from jax import lax
from jax.experimental import pallas as pl
from jax.experimental.pallas import tpu as pltpu
from jax.sharding import PartitionSpec as P

MESH = pl.DeviceIdType.MESH
F32 = jnp.float32
I32 = jnp.int32
VARS, NODES, LANES, HALO = 5, 64, 128, 32
SECTIONS, ROW, COLS = 4, 16, 8


def derivative_table():
    points = np.array([-1.0, -np.sqrt(0.2), np.sqrt(0.2), 1.0])
    weights = np.array([1.0 / np.prod([points[b] - points[c] for c in range(4) if c != b]) for b in range(4)])
    table = np.zeros((4, 4))
    for a in range(4):
        for b in range(4):
            if a != b:
                table[a, b] = weights[b] / weights[a] / (points[a] - points[b])
        table[a, a] = -np.sum(table[a])
    return table


def slope_matrix():
    table, eye = derivative_table().astype(np.float32).astype(np.float64), np.eye(4)
    parts = [np.eye(NODES)]
    for spots in ((table, eye, eye), (eye, table, eye), (eye, eye, table)):
        parts.append(np.kron(np.kron(spots[0], spots[1]), spots[2]))
    return np.concatenate(parts).astype(np.float32)


def dot(a, b):
    return jnp.dot(a, b, precision=lax.Precision.HIGHEST, preferred_element_type=F32)


def inverse_of(entries):
    left = [[entries[i][j] for j in range(4)] for i in range(4)]
    right = [[jnp.full_like(entries[0][0], 1.0 if i == j else 0.0) for j in range(4)] for i in range(4)]
    for pivot in range(4):
        scale = 1.0 / left[pivot][pivot]
        left[pivot] = [x * scale for x in left[pivot]]
        right[pivot] = [x * scale for x in right[pivot]]
        for target in range(4):
            if target != pivot:
                factor = left[target][pivot]
                left[target] = [x - factor * y for x, y in zip(left[target], left[pivot])]
                right[target] = [x - factor * y for x, y in zip(right[target], right[pivot])]
    return right


def pick(choices, which):
    out = choices[0]
    for i in range(1, len(choices)):
        out = jnp.where(which == i, choices[i], out)
    return out


def face_rows(u):
    sub = lax.broadcasted_iota(I32, (8, LANES), 0)
    low = sub < 4
    rows = [[u[0][0], u[0][1]], [u[3][0], u[3][1]], [], [], [], []]
    for h in range(2):
        a, b = u[2 * h], u[2 * h + 1]
        rows[2].append(jnp.where(low, a[0], pltpu.roll(b[0], 4, 0)))
        rows[3].append(jnp.where(low, pltpu.roll(a[1], 4, 0), b[1]))
    for f, k in ((4, 0), (5, 3)):
        at = k + 4 * (sub & 1)
        for h in range(2):
            a, b = u[2 * h], u[2 * h + 1]
            s = [jnp.take_along_axis(x, at, axis=0) for x in (a[0], a[1], b[0], b[1])]
            rows[f].append(jnp.where(low, jnp.where(sub < 2, s[0], s[1]), jnp.where(sub < 6, s[2], s[3])))
    return rows


def turned(a, b, code):
    swap = (code & 4) != 0
    a2 = jnp.where(swap, b, a)
    b2 = jnp.where(swap, a, b)
    a2 = jnp.where((code & 1) != 0, 3 - a2, a2)
    b2 = jnp.where((code & 2) != 0, 3 - b2, b2)
    return 4 * a2 + b2


def body(
    residual, transform, shifts, flux, penalty, block_inverse, nodal_inverse, neighbours, orientation, live_counts, slopes,
    out, rms,
    v_res, v_flux, v_pen, v_block, v_nodal, v_neigh, v_orient, v_slopes, s_transform, s_shift, s_live,
    n_all, mixed, blocks, pen_node, far_coef, far_row, own_at, halo_at, y, r, w, dirs, faces, near, pack, halo, red1, red2,
    in_sem, res_send, res_recv, pass_send, pass_recv, dir_send, dir_recv, across_send, across_recv, halo_send, halo_recv, red_send, red_recv, near_sem,
):
    s, e = lax.axis_index("section"), lax.axis_index("elem")
    x_peers = [(lax.rem(s + k, SECTIONS), e) for k in (1, 3, 2)]
    nxt, prv = (s, lax.rem(e + 1, 128)), (s, lax.rem(e + 127, 128))
    row_base = (e // ROW) * ROW
    row_at = e - row_base
    row_peers = [(s, row_base + lax.rem(row_at + k, ROW)) for k in (8, 9, 7, 6, 10, 5, 11, 4, 12, 3, 13, 2, 14, 15, 1)]
    plane_at = s * COLS + e // ROW
    plane_peers = []
    for k in (2, 1, 3, 0):
        for q in (4, 3, 5, 2, 6, 1, 7, 0):
            if k or q:
                plane_peers.append((lax.rem(s + k, SECTIONS), lax.rem(e + ROW * q, 128)))

    barrier = pltpu.get_barrier_semaphore()
    def along_row(k):
        return [(s, row_base + lax.rem(row_at + 2 * q, ROW)) for q in (k, COLS - k)]

    def along_column(k):
        return [(s, lax.rem(e + ROW * q, 128)) for q in (k, COLS - k)]

    peers = x_peers[:2] + [nxt, prv] + along_row(1) + along_column(1)
    for p in peers:
        pl.semaphore_signal(barrier, inc=1, device_id=p, device_id_type=MESH)
    rounds = [along_row(1), along_row(2), along_row(1), along_column(1), along_column(2), along_column(1)]

    def tell(n):
        for p in rounds[n]:
            pl.semaphore_signal(near_sem.at[n], inc=1, device_id=p, device_id_type=MESH)

    def hear(n):
        pl.semaphore_wait(near_sem.at[n], 2)


    loads = [
        (residual.at[0], v_res.at[s]), (flux, v_flux), (penalty, v_pen), (block_inverse, v_block), (nodal_inverse.at[0], v_nodal),
        (neighbours, v_neigh), (orientation, v_orient), (slopes, v_slopes), (transform, s_transform), (shifts, s_shift),
        (live_counts, s_live),
    ]
    loads = [pltpu.make_async_copy(a, b, in_sem.at[i]) for i, (a, b) in enumerate(loads)]
    for c in loads:
        c.start()

    pl.semaphore_wait(barrier, len(peers))
    sides = x_peers[:2]
    behind = [lax.rem(s + 3, SECTIONS), lax.rem(s + 1, SECTIONS)]
    res_copies = [[None] * VARS for _ in range(2)]
    for n in range(VARS):
        for d in range(2):
            k = n if d == 0 else VARS - 1 - n
            c = pltpu.make_async_remote_copy(
                src_ref=residual.at[0, k], dst_ref=v_res.at[s, k], send_sem=res_send.at[d, k], recv_sem=res_recv.at[d, k],
                device_id=sides[d], device_id_type=MESH,
            )
            c.start()
            res_copies[d][k] = c
    tell(0)
    for c in loads:
        c.wait()

    lane = lax.broadcasted_iota(I32, (8, LANES), 1)
    sub = lax.broadcasted_iota(I32, (8, LANES), 0)
    mask = jnp.where(lane < s_live[0], 1.0, 0.0).astype(F32)
    mask1 = mask[0:1]
    t_entries = [[jnp.full((8, LANES), s_transform[i, j], F32) for j in range(4)] for i in range(4)]
    inverse = inverse_of(t_entries)
    size = [jnp.maximum(sum(jnp.abs(x) for x in row), 1.0) for row in inverse]
    own_size = pick(size, s)
    scale = mask / own_size
    mix = [pick([inverse[i][t] for i in range(4)], s) * scale for t in range(4)]
    t_row = [pick([t_entries[i][t] for i in range(4)], s) * size[t] for t in range(4)]

    n_full = dot(v_slopes[...], v_nodal[...])
    n_high = n_full.astype(jnp.bfloat16)
    n_all[0:4 * NODES, :] = n_high
    n_all[4 * NODES:8 * NODES, :] = (n_full - n_high.astype(F32)).astype(jnp.bfloat16)

    def spread(k, x):
        high = x.astype(jnp.bfloat16)
        low = (x - high.astype(F32)).astype(jnp.bfloat16)
        first = jnp.dot(n_all[...], high, preferred_element_type=F32)
        second = jnp.dot(n_all[0:4 * NODES, :], low, preferred_element_type=F32)
        y[k] = first[0:4 * NODES] + (first[4 * NODES:8 * NODES] + second)

    for m in range(VARS):
        blocks[m] = jnp.concatenate([v_block[m, c] for c in range(VARS)], axis=0) * mask1
    for d in range(3):
        for k in range(VARS):
            total = None
            for m in range(VARS):
                term = v_flux[k, m, d:d + 1, :] * blocks[m]
                total = term if total is None else total + term
            mixed[d, k] = total

    hear(0)
    tell(1)
    passed = [[], []]
    for n in range(3):
        for d in range(2):
            k = n if d == 0 else VARS - 1 - n
            res_copies[d][k].wait_recv()
            rows = pl.ds(0, NODES) if n < 2 else pl.ds(NODES // 2 * d, NODES // 2)
            part = v_res.at[behind[d], k, rows]
            c = pltpu.make_async_remote_copy(
                src_ref=part, dst_ref=part, send_sem=pass_send.at[d, n], recv_sem=pass_recv.at[d, n], device_id=sides[d],
                device_id_type=MESH,
            )
            c.start()
            passed[d].append(c)
    hear(1)
    tell(2)
    dead = jnp.zeros((8, LANES), F32)
    coef, code = [], []
    for f in range(6):
        far = jnp.broadcast_to(v_neigh[f:f + 1, :], (8, LANES))
        there = far >= 0
        at = far - e * LANES
        inside = there & (at >= 0) & (at < LANES)
        before = there & (at < 0)
        after = there & (at >= LANES)
        own_at[f] = jnp.where(inside, at, 0)
        halo_at[f] = jnp.where(before, at + HALO, jnp.where(after, at - LANES, 0))
        halo_at[6 + f] = jnp.where(before, 1, jnp.where(after, 2, 0))
        coef.append(jnp.where(there, jnp.broadcast_to(v_pen[f:f + 1, :], (8, LANES)), dead) * mask)
        code.append(jnp.broadcast_to(v_orient[f:f + 1, :], (8, LANES)))
    k_at, j_low = sub & 3, sub >> 2
    for n, (i, jh) in enumerate(((0, 0), (0, 1), (3, 0), (3, 1))):
        f = 0 if i == 0 else 1
        far_coef[n] = coef[f]
        far_row[n] = turned(2 * jh + j_low, k_at, code[f])
    for i in range(4):
        for jh in range(2):
            n = 4 + 2 * i + jh
            f = 2 + jh
            far_coef[n] = jnp.where(j_low == jh, coef[f], dead)
            far_row[n] = turned(jnp.full((8, LANES), i, I32), k_at, code[f])
            n += 8
            low_face = k_at < 2
            far_coef[n] = jnp.where(k_at == 0, coef[4], jnp.where(k_at == 3, coef[5], dead))
            far_row[n] = turned(jnp.full((8, LANES), i, I32), 2 * jh + j_low, jnp.where(low_face, code[4], code[5]))
    own_pen = [jnp.broadcast_to(v_pen[f:f + 1, :], (8, LANES)) for f in range(6)]
    for i in range(4):
        for jh in range(2):
            total = jnp.full((8, LANES), s_shift[0], F32)
            if i in (0, 3):
                total = total + own_pen[0 if i == 0 else 1]
            total = total + jnp.where(j_low == jh, own_pen[2 + jh], dead)
            total = total + jnp.where(k_at == 0, own_pen[4], jnp.where(k_at == 3, own_pen[5], dead))
            pen_node[2 * i + jh] = total

    hear(2)
    tell(3)
    for k in (0, 4, 1, 3, 2):
        if k < 2:
            res_copies[1][k].wait_recv()
            passed[0][k].wait_recv()
        elif k > 2:
            res_copies[0][k].wait_recv()
            passed[1][VARS - 1 - k].wait_recv()
        else:
            passed[0][2].wait_recv()
            passed[1][2].wait_recv()
        for q in range(8):
            rows = pl.ds(8 * q, 8)
            total = mix[0] * v_res[0, k, rows, :]
            for t in range(1, 4):
                total = total + mix[t] * v_res[t, k, rows, :]
            r[k, rows, :] = total
        spread(k, r[k])

    dir_copies, across_copies, halo_copies = [], [], []

    def pass_on(step):
        for d in range(2):
            dir_copies[2 * step + d].wait_recv()
            part = dirs.at[step, behind[d], pl.ds(0, VARS), pl.ds(NODES // 2 * d, NODES // 2)]
            c = pltpu.make_async_remote_copy(
                src_ref=part, dst_ref=part, send_sem=across_send.at[step, d], recv_sem=across_recv.at[step, d],
                device_id=sides[d], device_id_type=MESH,
            )
            c.start()
            across_copies.append(c)

    sums = []

    def add_products(pairs):
        here = [None] * len(pairs)
        for k in range(VARS):
            for q in range(8):
                rows = pl.ds(8 * q, 8)
                v = {}
                for n in sorted({m for pair in pairs for m in pair}):
                    v[n] = r[k, rows, :] if n == 0 else w[n - 1, k, rows, :]
                for n, (i, j) in enumerate(pairs):
                    term = v[i] * v[j]
                    here[n] = term if here[n] is None else here[n] + term
        sums.extend(here)

    def operator(step, target):
        for k in range(VARS):
            total = None
            for c in range(VARS):
                term = blocks[k, c:c + 1, :] * y[c, 0:NODES, :]
                total = term if total is None else total + term
            dirs[step, s, k] = total
        for k in range(VARS):
            u = [[dirs[step, s, k, pl.ds(16 * i + 8 * jh, 8), :] for jh in range(2)] for i in range(4)]
            rows = face_rows(u)
            for f in range(6):
                for h in range(2):
                    faces[f * 10 + k * 2 + h] = rows[f][h]
        group = lane >> 5
        for p in range(15):
            x = [faces[4 * p + g] for g in range(4)]
            x = [x[0]] + [pltpu.roll(x[g], 32 * g, 1) for g in range(1, 4)]
            pack[step, 0, p] = jnp.where(group < 2, jnp.where(group == 0, x[0], x[1]), jnp.where(group == 2, x[2], x[3]))
            pack[step, 1, p] = jnp.where(group < 2, jnp.where(group == 0, x[1], x[2]), jnp.where(group == 2, x[3], x[0]))
        waits = []
        odd = lax.rem(e, 2)
        for side, p in ((odd, (s, lax.rem(e + 127 + 2 * odd, 128))), (1 - odd, (s, lax.rem(e + 1 + 126 * odd, 128)))):
            c = pltpu.make_async_remote_copy(
                src_ref=pack.at[step, side], dst_ref=halo.at[step, side], send_sem=halo_send.at[step, side],
                recv_sem=halo_recv.at[step, side], device_id=p, device_id_type=MESH,
            )
            c.start()
            waits.append(c)
            halo_copies.append(c)
        for d in range(2):
            c = pltpu.make_async_remote_copy(
                src_ref=dirs.at[step, s], dst_ref=dirs.at[step, s], send_sem=dir_send.at[step, d],
                recv_sem=dir_recv.at[step, d], device_id=sides[d], device_id_type=MESH,
            )
            c.start()
            dir_copies.append(c)
        if step == 1:
            pass_on(0)
        for k in range(VARS):
            total = jnp.concatenate([pen_node[q] for q in range(8)], axis=0) * dirs[step, s, k]
            for d in range(3):
                for c in range(VARS):
                    total = total + mixed[d, k, c:c + 1, :] * y[c, NODES * (d + 1):NODES * (d + 2), :]
            target[k] = total
        for f in range(6):
            at = own_at[f]
            for n in range(10):
                near[f * 10 + n] = jnp.take_along_axis(faces[(f ^ 1) * 10 + n], at, axis=1)
        if step == 1:
            add_products(((0, 0), (0, 1), (1, 1)))
        hear(3 + step)
        tell(4 + step)
        for c in waits:
            c.wait_recv()
        for f in range(6):
            at = halo_at[f]
            side = halo_at[6 + f]
            for n in range(10):
                m = (f ^ 1) * 10 + n
                p, g = m // 4, m % 4
                after = jnp.take_along_axis(halo[step, 0, p], at + 32 * g, axis=1)
                before = jnp.take_along_axis(halo[step, 1, p], at + 32 * ((g + 3) % 4), axis=1)
                near[f * 10 + n] = jnp.where(side == 0, near[f * 10 + n], jnp.where(side == 1, before, after))
        for n in range(20):
            row = far_row[n]
            at, high = row & 7, row >= 8
            if n < 4:
                f, i, jh = n // 2, 3 * (n // 2), n % 2
            else:
                i, jh = ((n - 4) % 8) // 2, n % 2
                f = 2 + jh if n < 12 else 4
            for k in range(VARS):
                def turn(face):
                    a = jnp.take_along_axis(near[face * 10 + 2 * k], at, axis=0)
                    b = jnp.take_along_axis(near[face * 10 + 2 * k + 1], at, axis=0)
                    return jnp.where(high, b, a)

                far = turn(f) if f < 4 else jnp.where(k_at < 2, turn(4), turn(5))
                rows = pl.ds(16 * i + 8 * jh, 8)
                target[k, rows, :] = target[k, rows, :] - far_coef[n] * far

    operator(0, w.at[0])
    for k in range(VARS):
        spread(k, w[0, k])
    operator(1, w.at[1])

    add_products(((0, 2), (1, 2), (2, 2)))
    stacked = dead
    for n in range(6):
        stacked = jnp.where(sub == n, jnp.sum(sums[n], axis=0, keepdims=True), stacked)
    stacked = jnp.where(sub == lane, jnp.sum(stacked, axis=1, keepdims=True), dead)
    hear(5)
    red1[row_at] = jnp.sum(stacked, axis=0, keepdims=True)
    for p in row_peers:
        pltpu.make_async_remote_copy(
            src_ref=red1.at[row_at], dst_ref=red1.at[row_at], send_sem=red_send.at[0], recv_sem=red_recv.at[0], device_id=p,
            device_id_type=MESH,
        ).start()
    all_row = pltpu.make_async_remote_copy(
        src_ref=red1.at[pl.ds(0, ROW - 1)], dst_ref=red1.at[pl.ds(0, ROW - 1)], send_sem=red_send.at[0],
        recv_sem=red_recv.at[0], device_id=prv, device_id_type=MESH,
    )
    pass_on(1)
    all_row.wait_recv()
    total = red1[0]
    for n in range(1, ROW):
        total = total + red1[n]
    red2[plane_at] = total
    for p in plane_peers:
        pltpu.make_async_remote_copy(
            src_ref=red2.at[plane_at], dst_ref=red2.at[plane_at], send_sem=red_send.at[1], recv_sem=red_recv.at[1],
            device_id=p, device_id_type=MESH,
        ).start()
    count = SECTIONS * COLS - 1
    all_plane = pltpu.make_async_remote_copy(
        src_ref=red2.at[pl.ds(0, count)], dst_ref=red2.at[pl.ds(0, count)], send_sem=red_send.at[1],
        recv_sem=red_recv.at[1], device_id=prv, device_id_type=MESH,
    )
    all_plane.wait_recv()
    totals = []
    for t in range(SECTIONS):
        total = red2[COLS * t]
        for n in range(1, COLS):
            total = total + red2[COLS * t + n]
        totals.append(total)
    totals = jnp.concatenate(totals, axis=0)
    g = [jnp.sum(jnp.where(lane[0:SECTIONS] == n, totals, 0.0), axis=1, keepdims=True) for n in range(6)]
    ratio = g[4] / g[2]
    c2 = (g[3] - ratio * g[1]) / (g[5] - ratio * g[4])
    c1 = g[1] / g[2] - ratio * c2
    one = [t_row[t] * c1[t:t + 1] for t in range(SECTIONS)]
    two = [t_row[t] * c2[t:t + 1] for t in range(SECTIONS)]
    start = jnp.sum(jnp.where(lax.broadcasted_iota(I32, (SECTIONS, 1), 0) == s, g[0], 0.0), axis=0, keepdims=True)
    rms[...] = own_size[0:1] * (jnp.sqrt(start) / np.float32(np.sqrt(np.float32(VARS * NODES * LANES * 128))))
    for c in across_copies:
        c.wait_recv()
    for k in range(VARS):
        for q in range(8):
            rows = pl.ds(8 * q, 8)
            total = None
            for t in range(SECTIONS):
                term = one[t] * dirs[0, t, k, rows, :] + two[t] * dirs[1, t, k, rows, :]
                total = term if total is None else total + term
            out[0, k, rows, :] = total
    for c in res_copies[0] + res_copies[1] + passed[0] + passed[1] + dir_copies + across_copies + halo_copies + [all_row, all_plane]:
        c.wait_send()


def local(*args):
    hbm = pl.BlockSpec(memory_space=pltpu.HBM)
    ANY = pl.BlockSpec(memory_space=pl.ANY)
    vmem = pl.BlockSpec(memory_space=pltpu.VMEM)
    dma = pltpu.SemaphoreType.DMA
    slopes = jnp.asarray(slope_matrix())
    args = list(args)
    args[3] = jnp.transpose(args[3], (1, 2, 0, 3))
    args[5] = jnp.transpose(args[5], (1, 2, 0, 3))
    update, rms = pl.pallas_call(
        body,
        out_shape=(
            pltpu.VMEM((1, VARS, NODES, LANES), F32),
            pltpu.VMEM((1, LANES), F32),
        ),
        in_specs=[hbm, hbm, ANY] + [hbm] * 6 + [ANY, hbm],
        out_specs=(vmem, vmem),
        scratch_shapes=[
            pltpu.VMEM((SECTIONS, VARS, NODES, LANES), F32),
            pltpu.VMEM((VARS, VARS, 3, LANES), F32),
            pltpu.VMEM((6, LANES), F32),
            pltpu.VMEM((VARS, VARS, 1, LANES), F32),
            pltpu.VMEM((NODES, NODES), F32),
            pltpu.VMEM((6, LANES), I32),
            pltpu.VMEM((6, LANES), I32),
            pltpu.VMEM((4 * NODES, NODES), F32),
            pltpu.SMEM((4, 4), F32),
            pltpu.SMEM((1,), F32),
            pltpu.SMEM((1,), I32),
            pltpu.VMEM((8 * NODES, NODES), jnp.bfloat16),
            pltpu.VMEM((3, VARS, VARS, LANES), F32),
            pltpu.VMEM((VARS, VARS, LANES), F32),
            pltpu.VMEM((8, 8, LANES), F32),
            pltpu.VMEM((20, 8, LANES), F32),
            pltpu.VMEM((20, 8, LANES), I32),
            pltpu.VMEM((6, 8, LANES), I32),
            pltpu.VMEM((12, 8, LANES), I32),
            pltpu.VMEM((VARS, 4 * NODES, LANES), F32),
            pltpu.VMEM((VARS, NODES, LANES), F32),
            pltpu.VMEM((2, VARS, NODES, LANES), F32),
            pltpu.VMEM((2, SECTIONS, VARS, NODES, LANES), F32),
            pltpu.VMEM((60, 8, LANES), F32),
            pltpu.VMEM((60, 8, LANES), F32),
            pltpu.VMEM((2, 2, 15, 8, LANES), F32),
            pltpu.VMEM((2, 2, 15, 8, LANES), F32),
            pltpu.VMEM((ROW, 1, LANES), F32),
            pltpu.VMEM((SECTIONS * COLS, 1, LANES), F32),
            dma((11,)), dma((2, VARS)), dma((2, VARS)), dma((2, 3)), dma((2, 3)), dma((2, 2)), dma((2, 2)), dma((2, 2)), dma((2, 2)),
            dma((2, 2)), dma((2, 2)), dma((2,)), dma((2,)), pltpu.SemaphoreType.REGULAR((6,)),
        ],
        compiler_params=pltpu.CompilerParams(collective_id=0, has_side_effects=True, vmem_limit_bytes=32 * 1024 * 1024),
        name="newton_step",
    )(*[x if x.shape == (1,) else pltpu.with_memory_space_constraint(x, pltpu.HBM) for x in args + [slopes]])
    return update, rms[0, 0:1]


def solution(mesh):
    placed = (
        P("section", None, None, "elem"), P(), P("section"), P(None, None, None, "elem"), P(None, "elem"),
        P("section", None, None, "elem"), P("section", None, None), P(None, "elem"), P(None, "elem"), P("elem"),
    )
    return jax.shard_map(
        local, mesh=mesh, in_specs=placed, out_specs=(P("section", None, None, "elem"), P("section")), check_vma=False,
    )
```

```python
import functools

import jax
import jax.numpy as jnp
import numpy as np
from jax import lax
from jax.experimental import pallas as pl
from jax.experimental.pallas import tpu as pltpu
from jax.sharding import PartitionSpec as P

MESH = pl.DeviceIdType.MESH
F32 = jnp.float32
I32 = jnp.int32
VARS, NODES, LANES, HALO = 5, 64, 128, 32
SECTIONS, ROW, COLS = 4, 16, 8


def derivative_table():
    points = np.array([-1.0, -np.sqrt(0.2), np.sqrt(0.2), 1.0])
    weights = np.array([1.0 / np.prod([points[b] - points[c] for c in range(4) if c != b]) for b in range(4)])
    table = np.zeros((4, 4))
    for a in range(4):
        for b in range(4):
            if a != b:
                table[a, b] = weights[b] / weights[a] / (points[a] - points[b])
        table[a, a] = -np.sum(table[a])
    return table


def slope_matrix():
    table, eye = derivative_table().astype(np.float32).astype(np.float64), np.eye(4)
    parts = [np.eye(NODES)]
    for spots in ((table, eye, eye), (eye, table, eye), (eye, eye, table)):
        parts.append(np.kron(np.kron(spots[0], spots[1]), spots[2]))
    return np.concatenate(parts).astype(np.float32)


def dot(a, b):
    return jnp.dot(a, b, precision=lax.Precision.HIGHEST, preferred_element_type=F32)


def inverse_of(entries):
    left = [[entries[i][j] for j in range(4)] for i in range(4)]
    right = [[jnp.full_like(entries[0][0], 1.0 if i == j else 0.0) for j in range(4)] for i in range(4)]
    for pivot in range(4):
        scale = 1.0 / left[pivot][pivot]
        left[pivot] = [x * scale for x in left[pivot]]
        right[pivot] = [x * scale for x in right[pivot]]
        for target in range(4):
            if target != pivot:
                factor = left[target][pivot]
                left[target] = [x - factor * y for x, y in zip(left[target], left[pivot])]
                right[target] = [x - factor * y for x, y in zip(right[target], right[pivot])]
    return right


def pick(choices, which):
    out = choices[0]
    for i in range(1, len(choices)):
        out = jnp.where(which == i, choices[i], out)
    return out


def face_rows(u):
    sub = lax.broadcasted_iota(I32, (8, LANES), 0)
    low = sub < 4
    rows = [[u[0][0], u[0][1]], [u[3][0], u[3][1]], [], [], [], []]
    for h in range(2):
        a, b = u[2 * h], u[2 * h + 1]
        rows[2].append(jnp.where(low, a[0], pltpu.roll(b[0], 4, 0)))
        rows[3].append(jnp.where(low, pltpu.roll(a[1], 4, 0), b[1]))
    for f, k in ((4, 0), (5, 3)):
        at = k + 4 * (sub & 1)
        for h in range(2):
            a, b = u[2 * h], u[2 * h + 1]
            s = [jnp.take_along_axis(x, at, axis=0) for x in (a[0], a[1], b[0], b[1])]
            rows[f].append(jnp.where(low, jnp.where(sub < 2, s[0], s[1]), jnp.where(sub < 6, s[2], s[3])))
    return rows


def turned(a, b, code):
    swap = (code & 4) != 0
    a2 = jnp.where(swap, b, a)
    b2 = jnp.where(swap, a, b)
    a2 = jnp.where((code & 1) != 0, 3 - a2, a2)
    b2 = jnp.where((code & 2) != 0, 3 - b2, b2)
    return 4 * a2 + b2


def body(
    residual, transform, shifts, flux, penalty, block_inverse, nodal_inverse, neighbours, orientation, live_counts, slopes,
    out, rms,
    v_res, v_flux, v_pen, v_block, v_nodal, v_neigh, v_orient, v_slopes, s_transform, s_shift, s_live,
    n_all, mixed, blocks, pen_node, far_coef, far_row, own_at, halo_at, y, r, w, dirs, faces, near, pack, halo, red1, red2,
    in_sem, res_send, res_recv, pass_send, pass_recv, dir_send, dir_recv, across_send, across_recv, halo_send, halo_recv, red_send, red_recv, near_sem,
):
    s, e = lax.axis_index("section"), lax.axis_index("elem")
    x_peers = [(lax.rem(s + k, SECTIONS), e) for k in (1, 3, 2)]
    nxt, prv = (s, lax.rem(e + 1, 128)), (s, lax.rem(e + 127, 128))
    row_base = (e // ROW) * ROW
    row_at = e - row_base
    row_peers = [(s, row_base + lax.rem(row_at + k, ROW)) for k in (8, 9, 7, 6, 10, 5, 11, 4, 12, 3, 13, 2, 14, 15, 1)]
    plane_at = s * COLS + e // ROW
    plane_peers = []
    for k in (2, 1, 3, 0):
        for q in (4, 3, 5, 2, 6, 1, 7, 0):
            if k or q:
                plane_peers.append((lax.rem(s + k, SECTIONS), lax.rem(e + ROW * q, 128)))

    barrier = pltpu.get_barrier_semaphore()
    def along_row(k):
        return [(s, row_base + lax.rem(row_at + 2 * q, ROW)) for q in (k, COLS - k)]

    def along_column(k):
        return [(s, lax.rem(e + ROW * q, 128)) for q in (k, COLS - k)]

    peers = x_peers[:2] + [nxt, prv] + along_row(1) + along_column(1)
    for p in peers:
        pl.semaphore_signal(barrier, inc=1, device_id=p, device_id_type=MESH)
    rounds = [along_row(1), along_row(2), along_row(1), along_column(1), along_column(2), along_column(1)]

    def tell(n):
        for p in rounds[n]:
            pl.semaphore_signal(near_sem.at[n], inc=1, device_id=p, device_id_type=MESH)

    def hear(n):
        pl.semaphore_wait(near_sem.at[n], 2)


    loads = [
        (residual.at[0], v_res.at[s]), (flux, v_flux), (penalty, v_pen), (block_inverse, v_block), (nodal_inverse.at[0], v_nodal),
        (neighbours, v_neigh), (orientation, v_orient), (slopes, v_slopes), (transform, s_transform), (shifts, s_shift),
        (live_counts, s_live),
    ]
    loads = [pltpu.make_async_copy(a, b, in_sem.at[i]) for i, (a, b) in enumerate(loads)]
    for c in loads:
        c.start()

    pl.semaphore_wait(barrier, len(peers))
    sides = x_peers[:2]
    behind = [lax.rem(s + 3, SECTIONS), lax.rem(s + 1, SECTIONS)]
    res_copies = [[None] * VARS for _ in range(2)]
    for n in range(VARS):
        for d in range(2):
            k = n if d == 0 else VARS - 1 - n
            c = pltpu.make_async_remote_copy(
                src_ref=residual.at[0, k], dst_ref=v_res.at[s, k], send_sem=res_send.at[d, k], recv_sem=res_recv.at[d, k],
                device_id=sides[d], device_id_type=MESH,
            )
            c.start()
            res_copies[d][k] = c
    tell(0)
    for c in loads:
        c.wait()

    lane = lax.broadcasted_iota(I32, (8, LANES), 1)
    sub = lax.broadcasted_iota(I32, (8, LANES), 0)
    mask = jnp.where(lane < s_live[0], 1.0, 0.0).astype(F32)
    mask1 = mask[0:1]
    t_entries = [[jnp.full((8, LANES), s_transform[i, j], F32) for j in range(4)] for i in range(4)]
    inverse = inverse_of(t_entries)
    size = [jnp.maximum(sum(jnp.abs(x) for x in row), 1.0) for row in inverse]
    own_size = pick(size, s)
    scale = mask / own_size
    mix = [pick([inverse[i][t] for i in range(4)], s) * scale for t in range(4)]
    t_row = [pick([t_entries[i][t] for i in range(4)], s) * size[t] for t in range(4)]

    n_full = dot(v_slopes[...], v_nodal[...])
    n_high = n_full.astype(jnp.bfloat16)
    n_all[0:4 * NODES, :] = n_high
    n_all[4 * NODES:8 * NODES, :] = (n_full - n_high.astype(F32)).astype(jnp.bfloat16)

    def spread(k, x):
        high = x.astype(jnp.bfloat16)
        low = (x - high.astype(F32)).astype(jnp.bfloat16)
        first = jnp.dot(n_all[...], high, preferred_element_type=F32)
        second = jnp.dot(n_all[0:4 * NODES, :], low, preferred_element_type=F32)
        y[k] = first[0:4 * NODES] + (first[4 * NODES:8 * NODES] + second)

    for m in range(VARS):
        blocks[m] = jnp.concatenate([v_block[m, c] for c in range(VARS)], axis=0) * mask1
    for d in range(3):
        for k in range(VARS):
            total = None
            for m in range(VARS):
                term = v_flux[k, m, d:d + 1, :] * blocks[m]
                total = term if total is None else total + term
            mixed[d, k] = total

    hear(0)
    tell(1)
    passed = [[], []]
    for n in range(3):
        for d in range(2):
            k = n if d == 0 else VARS - 1 - n
            res_copies[d][k].wait_recv()
            rows = pl.ds(0, NODES) if n < 2 else pl.ds(NODES // 2 * d, NODES // 2)
            part = v_res.at[behind[d], k, rows]
            c = pltpu.make_async_remote_copy(
                src_ref=part, dst_ref=part, send_sem=pass_send.at[d, n], recv_sem=pass_recv.at[d, n], device_id=sides[d],
                device_id_type=MESH,
            )
            c.start()
            passed[d].append(c)
    hear(1)
    tell(2)
    dead = jnp.zeros((8, LANES), F32)
    coef, code = [], []
    for f in range(6):
        far = jnp.broadcast_to(v_neigh[f:f + 1, :], (8, LANES))
        there = far >= 0
        at = far - e * LANES
        inside = there & (at >= 0) & (at < LANES)
        before = there & (at < 0)
        after = there & (at >= LANES)
        own_at[f] = jnp.where(inside, at, 0)
        halo_at[f] = jnp.where(before, at + HALO, jnp.where(after, at - LANES, 0))
        halo_at[6 + f] = jnp.where(before, 1, jnp.where(after, 2, 0))
        coef.append(jnp.where(there, jnp.broadcast_to(v_pen[f:f + 1, :], (8, LANES)), dead) * mask)
        code.append(jnp.broadcast_to(v_orient[f:f + 1, :], (8, LANES)))
    k_at, j_low = sub & 3, sub >> 2
    for n, (i, jh) in enumerate(((0, 0), (0, 1), (3, 0), (3, 1))):
        f = 0 if i == 0 else 1
        far_coef[n] = coef[f]
        far_row[n] = turned(2 * jh + j_low, k_at, code[f])
    for i in range(4):
        for jh in range(2):
            n = 4 + 2 * i + jh
            f = 2 + jh
            far_coef[n] = jnp.where(j_low == jh, coef[f], dead)
            far_row[n] = turned(jnp.full((8, LANES), i, I32), k_at, code[f])
            n += 8
            low_face = k_at < 2
            far_coef[n] = jnp.where(k_at == 0, coef[4], jnp.where(k_at == 3, coef[5], dead))
            far_row[n] = turned(jnp.full((8, LANES), i, I32), 2 * jh + j_low, jnp.where(low_face, code[4], code[5]))
    own_pen = [jnp.broadcast_to(v_pen[f:f + 1, :], (8, LANES)) for f in range(6)]
    for i in range(4):
        for jh in range(2):
            total = jnp.full((8, LANES), s_shift[0], F32)
            if i in (0, 3):
                total = total + own_pen[0 if i == 0 else 1]
            total = total + jnp.where(j_low == jh, own_pen[2 + jh], dead)
            total = total + jnp.where(k_at == 0, own_pen[4], jnp.where(k_at == 3, own_pen[5], dead))
            pen_node[2 * i + jh] = total

    hear(2)
    tell(3)
    for k in (0, 4, 1, 3, 2):
        if k < 2:
            res_copies[1][k].wait_recv()
            passed[0][k].wait_recv()
        elif k > 2:
            res_copies[0][k].wait_recv()
            passed[1][VARS - 1 - k].wait_recv()
        else:
            passed[0][2].wait_recv()
            passed[1][2].wait_recv()
        for q in range(8):
            rows = pl.ds(8 * q, 8)
            total = mix[0] * v_res[0, k, rows, :]
            for t in range(1, 4):
                total = total + mix[t] * v_res[t, k, rows, :]
            r[k, rows, :] = total
        spread(k, r[k])

    dir_copies, across_copies, halo_copies = [], [], []

    def pass_on(step):
        for d in range(2):
            dir_copies[2 * step + d].wait_recv()
            part = dirs.at[step, behind[d], pl.ds(0, VARS), pl.ds(NODES // 2 * d, NODES // 2)]
            c = pltpu.make_async_remote_copy(
                src_ref=part, dst_ref=part, send_sem=across_send.at[step, d], recv_sem=across_recv.at[step, d],
                device_id=sides[d], device_id_type=MESH,
            )
            c.start()
            across_copies.append(c)

    sums = []

    def add_products(pairs):
        here = [None] * len(pairs)
        for k in range(VARS):
            for q in range(8):
                rows = pl.ds(8 * q, 8)
                v = {}
                for n in sorted({m for pair in pairs for m in pair}):
                    v[n] = r[k, rows, :] if n == 0 else w[n - 1, k, rows, :]
                for n, (i, j) in enumerate(pairs):
                    term = v[i] * v[j]
                    here[n] = term if here[n] is None else here[n] + term
        sums.extend(here)

    def operator(step, target):
        for k in range(VARS):
            total = None
            for c in range(VARS):
                term = blocks[k, c:c + 1, :] * y[c, 0:NODES, :]
                total = term if total is None else total + term
            dirs[step, s, k] = total
        for k in range(VARS):
            u = [[dirs[step, s, k, pl.ds(16 * i + 8 * jh, 8), :] for jh in range(2)] for i in range(4)]
            rows = face_rows(u)
            for f in range(6):
                for h in range(2):
                    faces[f * 10 + k * 2 + h] = rows[f][h]
        group = lane >> 5
        for p in range(15):
            x = [faces[4 * p + g] for g in range(4)]
            x = [x[0]] + [pltpu.roll(x[g], 32 * g, 1) for g in range(1, 4)]
            pack[step, 0, p] = jnp.where(group < 2, jnp.where(group == 0, x[0], x[1]), jnp.where(group == 2, x[2], x[3]))
            pack[step, 1, p] = jnp.where(group < 2, jnp.where(group == 0, x[1], x[2]), jnp.where(group == 2, x[3], x[0]))
        waits = []
        for side, p in ((0, prv), (1, nxt)):
            c = pltpu.make_async_remote_copy(
                src_ref=pack.at[step, side], dst_ref=halo.at[step, side], send_sem=halo_send.at[step, side],
                recv_sem=halo_recv.at[step, side], device_id=p, device_id_type=MESH,
            )
            c.start()
            waits.append(c)
            halo_copies.append(c)
        for d in range(2):
            c = pltpu.make_async_remote_copy(
                src_ref=dirs.at[step, s], dst_ref=dirs.at[step, s], send_sem=dir_send.at[step, d],
                recv_sem=dir_recv.at[step, d], device_id=sides[d], device_id_type=MESH,
            )
            c.start()
            dir_copies.append(c)
        if step == 1:
            pass_on(0)
        for k in range(VARS):
            total = jnp.concatenate([pen_node[q] for q in range(8)], axis=0) * dirs[step, s, k]
            for d in range(3):
                for c in range(VARS):
                    total = total + mixed[d, k, c:c + 1, :] * y[c, NODES * (d + 1):NODES * (d + 2), :]
            target[k] = total
        for f in range(6):
            at = own_at[f]
            for n in range(10):
                near[f * 10 + n] = jnp.take_along_axis(faces[(f ^ 1) * 10 + n], at, axis=1)
        if step == 1:
            add_products(((0, 0), (0, 1), (1, 1)))
        hear(3 + step)
        tell(4 + step)
        for c in waits:
            c.wait_recv()
        for f in range(6):
            at = halo_at[f]
            side = halo_at[6 + f]
            for n in range(10):
                m = (f ^ 1) * 10 + n
                p, g = m // 4, m % 4
                after = jnp.take_along_axis(halo[step, 0, p], at + 32 * g, axis=1)
                before = jnp.take_along_axis(halo[step, 1, p], at + 32 * ((g + 3) % 4), axis=1)
                near[f * 10 + n] = jnp.where(side == 0, near[f * 10 + n], jnp.where(side == 1, before, after))
        for n in range(20):
            row = far_row[n]
            at, high = row & 7, row >= 8
            if n < 4:
                f, i, jh = n // 2, 3 * (n // 2), n % 2
            else:
                i, jh = ((n - 4) % 8) // 2, n % 2
                f = 2 + jh if n < 12 else 4
            for k in range(VARS):
                def turn(face):
                    a = jnp.take_along_axis(near[face * 10 + 2 * k], at, axis=0)
                    b = jnp.take_along_axis(near[face * 10 + 2 * k + 1], at, axis=0)
                    return jnp.where(high, b, a)

                far = turn(f) if f < 4 else jnp.where(k_at < 2, turn(4), turn(5))
                rows = pl.ds(16 * i + 8 * jh, 8)
                target[k, rows, :] = target[k, rows, :] - far_coef[n] * far

    operator(0, w.at[0])
    for k in range(VARS):
        spread(k, w[0, k])
    operator(1, w.at[1])

    add_products(((0, 2), (1, 2), (2, 2)))
    stacked = dead
    for n in range(6):
        stacked = jnp.where(sub == n, jnp.sum(sums[n], axis=0, keepdims=True), stacked)
    stacked = jnp.where(sub == lane, jnp.sum(stacked, axis=1, keepdims=True), dead)
    hear(5)
    red1[row_at] = jnp.sum(stacked, axis=0, keepdims=True)
    for p in row_peers:
        pltpu.make_async_remote_copy(
            src_ref=red1.at[row_at], dst_ref=red1.at[row_at], send_sem=red_send.at[0], recv_sem=red_recv.at[0], device_id=p,
            device_id_type=MESH,
        ).start()
    all_row = pltpu.make_async_remote_copy(
        src_ref=red1.at[pl.ds(0, ROW - 1)], dst_ref=red1.at[pl.ds(0, ROW - 1)], send_sem=red_send.at[0],
        recv_sem=red_recv.at[0], device_id=prv, device_id_type=MESH,
    )
    pass_on(1)
    all_row.wait_recv()
    total = red1[0]
    for n in range(1, ROW):
        total = total + red1[n]
    red2[plane_at] = total
    for p in plane_peers:
        pltpu.make_async_remote_copy(
            src_ref=red2.at[plane_at], dst_ref=red2.at[plane_at], send_sem=red_send.at[1], recv_sem=red_recv.at[1],
            device_id=p, device_id_type=MESH,
        ).start()
    count = SECTIONS * COLS - 1
    all_plane = pltpu.make_async_remote_copy(
        src_ref=red2.at[pl.ds(0, count)], dst_ref=red2.at[pl.ds(0, count)], send_sem=red_send.at[1],
        recv_sem=red_recv.at[1], device_id=prv, device_id_type=MESH,
    )
    all_plane.wait_recv()
    totals = []
    for t in range(SECTIONS):
        total = red2[COLS * t]
        for n in range(1, COLS):
            total = total + red2[COLS * t + n]
        totals.append(total)
    totals = jnp.concatenate(totals, axis=0)
    g = [jnp.sum(jnp.where(lane[0:SECTIONS] == n, totals, 0.0), axis=1, keepdims=True) for n in range(6)]
    ratio = g[4] / g[2]
    c2 = (g[3] - ratio * g[1]) / (g[5] - ratio * g[4])
    c1 = g[1] / g[2] - ratio * c2
    one = [t_row[t] * c1[t:t + 1] for t in range(SECTIONS)]
    two = [t_row[t] * c2[t:t + 1] for t in range(SECTIONS)]
    start = jnp.sum(jnp.where(lax.broadcasted_iota(I32, (SECTIONS, 1), 0) == s, g[0], 0.0), axis=0, keepdims=True)
    rms[...] = own_size[0:1] * (jnp.sqrt(start) / np.float32(np.sqrt(np.float32(VARS * NODES * LANES * 128))))
    for c in across_copies:
        c.wait_recv()
    for k in range(VARS):
        for q in range(8):
            rows = pl.ds(8 * q, 8)
            total = None
            for t in range(SECTIONS):
                term = one[t] * dirs[0, t, k, rows, :] + two[t] * dirs[1, t, k, rows, :]
                total = term if total is None else total + term
            out[0, k, rows, :] = total
    for c in res_copies[0] + res_copies[1] + passed[0] + passed[1] + dir_copies + across_copies + halo_copies + [all_row, all_plane]:
        c.wait_send()


def local(*args):
    hbm = pl.BlockSpec(memory_space=pltpu.HBM)
    ANY = pl.BlockSpec(memory_space=pl.ANY)
    vmem = pl.BlockSpec(memory_space=pltpu.VMEM)
    dma = pltpu.SemaphoreType.DMA
    slopes = jnp.asarray(slope_matrix())
    args = list(args)
    args[3] = jnp.transpose(args[3], (1, 2, 0, 3))
    args[5] = jnp.transpose(args[5], (1, 2, 0, 3))
    update, rms = pl.pallas_call(
        body,
        out_shape=(
            pltpu.VMEM((1, VARS, NODES, LANES), F32),
            pltpu.VMEM((1, LANES), F32),
        ),
        in_specs=[hbm, hbm, ANY] + [hbm] * 6 + [ANY, hbm],
        out_specs=(vmem, vmem),
        scratch_shapes=[
            pltpu.VMEM((SECTIONS, VARS, NODES, LANES), F32),
            pltpu.VMEM((VARS, VARS, 3, LANES), F32),
            pltpu.VMEM((6, LANES), F32),
            pltpu.VMEM((VARS, VARS, 1, LANES), F32),
            pltpu.VMEM((NODES, NODES), F32),
            pltpu.VMEM((6, LANES), I32),
            pltpu.VMEM((6, LANES), I32),
            pltpu.VMEM((4 * NODES, NODES), F32),
            pltpu.SMEM((4, 4), F32),
            pltpu.SMEM((1,), F32),
            pltpu.SMEM((1,), I32),
            pltpu.VMEM((8 * NODES, NODES), jnp.bfloat16),
            pltpu.VMEM((3, VARS, VARS, LANES), F32),
            pltpu.VMEM((VARS, VARS, LANES), F32),
            pltpu.VMEM((8, 8, LANES), F32),
            pltpu.VMEM((20, 8, LANES), F32),
            pltpu.VMEM((20, 8, LANES), I32),
            pltpu.VMEM((6, 8, LANES), I32),
            pltpu.VMEM((12, 8, LANES), I32),
            pltpu.VMEM((VARS, 4 * NODES, LANES), F32),
            pltpu.VMEM((VARS, NODES, LANES), F32),
            pltpu.VMEM((2, VARS, NODES, LANES), F32),
            pltpu.VMEM((2, SECTIONS, VARS, NODES, LANES), F32),
            pltpu.VMEM((60, 8, LANES), F32),
            pltpu.VMEM((60, 8, LANES), F32),
            pltpu.VMEM((2, 2, 15, 8, LANES), F32),
            pltpu.VMEM((2, 2, 15, 8, LANES), F32),
            pltpu.VMEM((ROW, 1, LANES), F32),
            pltpu.VMEM((SECTIONS * COLS, 1, LANES), F32),
            dma((11,)), dma((2, VARS)), dma((2, VARS)), dma((2, 3)), dma((2, 3)), dma((2, 2)), dma((2, 2)), dma((2, 2)), dma((2, 2)),
            dma((2, 2)), dma((2, 2)), dma((2,)), dma((2,)), pltpu.SemaphoreType.REGULAR((6,)),
        ],
        compiler_params=pltpu.CompilerParams(collective_id=0, has_side_effects=True, vmem_limit_bytes=32 * 1024 * 1024),
        name="newton_step",
    )(*[x if x.shape == (1,) else pltpu.with_memory_space_constraint(x, pltpu.HBM) for x in args + [slopes]])
    return update, rms[0, 0:1]


def solution(mesh):
    placed = (
        P("section", None, None, "elem"), P(), P("section"), P(None, None, None, "elem"), P(None, "elem"),
        P("section", None, None, "elem"), P("section", None, None), P(None, "elem"), P(None, "elem"), P("elem"),
    )
    return jax.shard_map(
        local, mesh=mesh, in_specs=placed, out_specs=(P("section", None, None, "elem"), P("section")), check_vma=False,
    )
```
